256 devices in a mesh: visit: 64 (over z, x, core), band: 4 (over y).
Axes of the slice: x: 4, y: 4, z: 8, core: 2. Of those that a mesh axis runs over, the one named last changes fastest.
Arguments:
- source: bfloat16 [64, 2, 160, 8448], P('visit', None, 'band'), may hold values from -6 to 6
- row_start: int32 [64, 128], P('visit', 'band'), may hold values from 0 to 36
- row_weight: bfloat16 [64, 4, 128], P('visit', None, 'band'), may hold values from -0.25 to 0.75
- col_start: int32 [64, 8192], P('visit'), may hold values from 0 to 252
- col_weight: bfloat16 [64, 4, 8192], P('visit'), may hold values from -0.25 to 0.75
- col_offset: int32 [64, 64], P('visit'), may hold values from 0 to 127
- g_taps: bfloat16 [16, 21], replicated, may hold values from -1.25 to 1.25
- h_taps: bfloat16 [16, 21], replicated, may hold values from -1.25 to 1.25
- coef_table: float32 [16, 16, 6], replicated, may hold values from -1.5 to 1.5
- table_ids: int32 [64, 2], P('visit'), may hold values from 0 to 15
- vis_weight: float32 [64, 2], replicated, may hold values from 0.1 to 10
- coverage: int32 [64, 64], replicated, may hold values from 0 to 1, as said below
Outputs:
- coadd: float32 [2, 128, 8192], P(None, 'band', 'visit')
The draws below stay inside these ranges and needn't reach their ends.
Inputs may be any that keep to these rules, and one draw needn't show every extreme that they name: `coverage`: each visit misses one run of consecutive patches, wrapping, of length 0 to 32, and always intersects the patch of its own index.
All inputs are finite; a program needn't handle non-finite values.
Results may differ from the reference program's by a relative error of at most 0.0057.
Values may be sent and summed in bfloat16 or wider, within the bound.
No kernel may reach another device: no remote copies, remote signals or barrier semaphores. Data moves between devices by JAX's collectives and lax.ppermute only.
A program may use at most 128 MiB of HBM per device.

```python
import math
import jax
import jax.numpy as jnp
from jax import lax

NB = 2
NBASIS = 16
KTAPS = 21
NPOLY = 6
NTAB = 16
CBW = 128
RB = 32
PC = 128
SR = 40
NR = 128
NSR = 160
PATCHES = 64
VISITS = 64
NCOL = 8192
CB = 64
SC = 8448


def draw_coverage(key, part):
    key = jax.random.fold_in(key, 7)
    missing = jax.random.randint(key, (VISITS, 1), 0, PATCHES // 2 + 1)
    relative = (jnp.arange(PATCHES, dtype=jnp.int32)[None, :] - jnp.arange(VISITS, dtype=jnp.int32)[:, None] - 1) % PATCHES
    return (relative >= missing).astype(jnp.int32)


def place_ends(entries, own_key, smallest, top_value):
    shape = entries.shape
    spot = [jax.random.randint(jax.random.fold_in(own_key, axis), (), 0, shape[axis]) for axis in range(len(shape))]
    entries = entries.at[tuple(spot)].set(smallest)
    longest = shape.index(max(shape))
    spot[longest] = (spot[longest] + 1) % shape[longest]
    return entries.at[tuple(spot)].set(top_value)


def block_levels(own_key, extent, pieces, smallest, largest):
    loudness, own = 1.0, jax.random.fold_in(own_key, 6)
    for dim, blocks in pieces:
        draws = jnp.exp(jax.random.uniform(jax.random.fold_in(own, dim), (blocks,), jnp.float32, smallest / len(pieces), largest / len(pieces)))
        loudness = loudness * jnp.repeat(draws, extent[dim] // blocks).reshape([-1 if axis == dim else 1 for axis in range(len(extent))])
    return loudness


def normal_values(rng, shape, scale, bound, split=(), kind=jnp.bfloat16):
    result = jax.random.normal(rng, shape, jnp.float32) * scale
    if len(split) > 0:
        result = block_levels(rng, shape, split, -0.22, 0.18) * result
    return jnp.clip(result, min=-bound, max=bound).astype(kind)


def setup_inputs(seed: int = 0) -> dict:
    splits = jax.random.split(jax.random.key(seed), 13)
    source = normal_values(splits[0], (VISITS, NB, NSR, SC), 1.0, 6.0, ((0, 64), (2, 4)))
    row_start = place_ends(jax.random.randint(splits[1], (VISITS, NR), 0, SR - 3), jax.random.fold_in(splits[1], 1), 0, (SR - 3) - 1).astype(jnp.int32)
    row_weight = jnp.clip(-0.25 + 1.0 * jax.random.uniform(splits[2], (VISITS, 4, NR), jnp.float32) ** block_levels(splits[2], (VISITS, 4, NR), ((0, 64), (2, 4)), -0.2, 0.2), -0.25, 0.75).astype(jnp.bfloat16)
    col_start = place_ends(jax.random.randint(splits[3], (VISITS, NCOL), 0, 2 * CBW - 3), jax.random.fold_in(splits[3], 1), 0, (2 * CBW - 3) - 1).astype(jnp.int32)
    col_weight = jnp.clip(-0.25 + 1.0 * jax.random.uniform(splits[4], (VISITS, 4, NCOL), jnp.float32) ** block_levels(splits[4], (VISITS, 4, NCOL), ((0, 64),), -0.2, 0.2), -0.25, 0.75).astype(jnp.bfloat16)
    col_offset = place_ends(jax.random.randint(splits[5], (VISITS, CB), 0, CBW), jax.random.fold_in(splits[5], 1), 0, CBW - 1).astype(jnp.int32)
    g_taps = normal_values(splits[6], (NBASIS, KTAPS), KTAPS ** -0.5, 1.25)
    h_taps = normal_values(splits[7], (NBASIS, KTAPS), KTAPS ** -0.5, 1.25)
    coef_table = normal_values(splits[8], (NTAB, NBASIS, NPOLY), NBASIS ** -0.5, 1.5, (), jnp.float32)
    table_ids = place_ends(jax.random.randint(splits[9], (VISITS, NB), 0, NTAB), jax.random.fold_in(splits[9], 1), 0, NTAB - 1).astype(jnp.int32)
    vis_weight = jnp.clip(jnp.exp(jax.random.uniform(splits[10], (VISITS, NB), jnp.float32, math.log(0.1), math.log(10.0))), 0.1, 10.0)
    coverage = draw_coverage(jax.random.fold_in(splits[12], 71), 0)
    return dict(source=source, row_start=row_start, row_weight=row_weight, col_start=col_start, col_weight=col_weight, col_offset=col_offset, g_taps=g_taps, h_taps=h_taps, coef_table=coef_table, table_ids=table_ids, vis_weight=vis_weight, coverage=coverage)


def coordinates(count):
    return (jnp.arange(count, dtype=jnp.float32) + 0.5) * (2.0 / count) - 1.0


def reference(source, row_start, row_weight, col_start, col_weight, col_offset, g_taps, h_taps, coef_table, table_ids, vis_weight, coverage):
    margin = KTAPS // 2
    rows_total = row_start.shape[1]
    cols_total = col_start.shape[1]
    row_block = jnp.arange(rows_total, dtype=jnp.int32) // RB
    col_block = jnp.arange(cols_total, dtype=jnp.int32) // CBW
    col_patch = jnp.arange(cols_total, dtype=jnp.int32) // PC
    ycoord = coordinates(rows_total)[:, None] * jnp.ones((1, cols_total), jnp.float32)
    xcoord = jnp.ones((rows_total, 1), jnp.float32) * coordinates(cols_total)[None, :]
    polys = jnp.stack([jnp.ones_like(xcoord), xcoord, ycoord, xcoord * xcoord, xcoord * ycoord, ycoord * ycoord])
    g_float = g_taps.astype(jnp.float32)
    h_float = h_taps.astype(jnp.float32)
    cover_float = coverage.astype(jnp.float32)

    def visit_step(total, visit):
        image = source[visit]
        row_index = (row_block * SR + row_start[visit]).astype(jnp.int32)
        row_wts = row_weight[visit].astype(jnp.float32)
        rowres = sum(row_wts[shift][None, :, None] * image[:, row_index + shift, :].astype(jnp.float32) for shift in range(4))
        rowres = rowres.astype(jnp.bfloat16)
        col_index = (col_block * CBW + col_offset[visit][col_block] + col_start[visit]).astype(jnp.int32)
        col_wts = col_weight[visit].astype(jnp.float32)
        resampled = sum(col_wts[shift][None, None, :] * rowres[:, :, col_index + shift].astype(jnp.float32) for shift in range(4))
        resampled = lax.optimization_barrier(resampled.astype(jnp.bfloat16)).astype(jnp.float32)
        padded = jnp.pad(resampled, ((0, 0), (0, 0), (margin, margin)))
        across = sum(h_float[:, shift][None, :, None, None] * padded[:, None, :, shift:shift + cols_total] for shift in range(KTAPS))
        across = lax.optimization_barrier(across.astype(jnp.bfloat16)).astype(jnp.float32)
        padded_rows = jnp.pad(across, ((0, 0), (0, 0), (margin, margin), (0, 0)))
        smooth = sum(g_float[:, shift][None, :, None, None] * padded_rows[:, :, shift:shift + rows_total, :] for shift in range(KTAPS))
        coefs = coef_table[table_ids[visit]]
        inner = jnp.einsum('nbt,nbik->ntik', coefs, smooth, precision=lax.Precision.HIGHEST)
        matched = jnp.sum(polys[None] * inner, axis=1)
        matched = lax.optimization_barrier(matched.astype(jnp.bfloat16)).astype(jnp.float32)
        factor = cover_float[visit][col_patch][None, :] * vis_weight[visit][:, None]
        return total + factor[:, None, :] * matched, None

    start = jnp.zeros((NB, rows_total, cols_total), jnp.float32)
    total, _ = lax.scan(visit_step, start, jnp.arange(VISITS, dtype=jnp.int32))
    denom = jnp.einsum('vj,vn->nj', cover_float, vis_weight, precision=lax.Precision.HIGHEST)
    return total / denom[:, col_patch][:, None, :]
```

```python
import jax
import jax.numpy as jnp
from jax import lax
from jax.sharding import PartitionSpec as P
from jax.experimental import pallas as pl
from jax.experimental.pallas import tpu as pltpu

F32 = jnp.float32
BF16 = jnp.bfloat16
HIGH = lax.Precision.HIGHEST

NB = 2
RB = 32
SR = 40
LANES = 128
ZN, XN, CN = 8, 4, 2
GROUP = XN * CN
GW = GROUP * LANES
HALO = 24
OR = RB + HALO
PR = NB * OR
HALF = LANES // 2


def iota(shape, dim):
    return lax.broadcasted_iota(jnp.int32, shape, dim)


def mm(a, b):
    return jnp.dot(a, b, preferred_element_type=F32)


def compute_kernel(
    off_ref,
    ids_ref,
    source_ref,
    row_start_ref,
    row_weight_ref,
    col_start_ref,
    col_weight_ref,
    g_ref,
    h_ref,
    coef_ref,
    weight_ref,
    cover_ref,
    keep_ref,
    send_ref,
    rowres_ref,
    shifted_ref,
    toep_ref,
    rows_ref,
    scale_ref,
    across_ref,
):
    visit = lax.axis_index("visit")
    band = lax.axis_index("band")
    core = visit % CN
    my_x = (visit // CN) % XN
    my_z = visit // GROUP
    taps = g_ref.shape[1]
    margin = taps // 2
    basis = g_ref.shape[0]
    blocks = off_ref.shape[1]
    width = blocks * LANES
    visits = cover_ref.shape[0]

    start = row_start_ref[...]
    weights = row_weight_ref[0].astype(F32)
    rel = iota((SR, RB), 0) - start
    picked = jnp.zeros((SR, RB), F32)
    for q in range(4):
        picked = jnp.where(rel == q, weights[q : q + 1, :], picked)
    picker = picked.T.astype(BF16)
    chunk = 2 * LANES

    def row_step(j, _):
        cols = pl.ds(pl.multiple_of(j * chunk, chunk), chunk)
        for n in range(NB):
            rowres_ref[n * RB : (n + 1) * RB, cols] = mm(
                picker, source_ref[0, n, :, cols]
            ).astype(BF16)
        return 0

    lax.fori_loop(0, rowres_ref.shape[1] // chunk, row_step, 0, unroll=3)

    low = iota((NB * RB, LANES), 1) < HALF
    tall = 3 * LANES
    tall_iota = iota((tall, LANES), 0)

    def col_step(c, before):
        first = pl.multiple_of(c * LANES, LANES)
        cols = pl.ds(first, LANES)
        at = col_start_ref[0:1, cols] + off_ref[0, c]
        wts = col_weight_ref[0, :, cols].astype(F32)
        rel = tall_iota - at
        spread = jnp.zeros((tall, LANES), F32)
        for q in range(4):
            spread = jnp.where(rel == q, wts[q : q + 1, :], spread)
        res = mm(rowres_ref[:, pl.ds(first, tall)], spread.astype(BF16))
        rolled = pltpu.roll(res, HALF, 1)
        shifted_ref[:, cols] = jnp.where(low, before, rolled).astype(BF16)
        return rolled

    last = lax.fori_loop(0, blocks, col_step, jnp.zeros((NB * RB, LANES), F32), unroll=4)
    shifted_ref[:, width : width + LANES] = jnp.where(low, last, 0.0).astype(BF16)

    tap = iota((2 * LANES, LANES), 0) - iota((2 * LANES, LANES), 1) - (HALF - margin)
    h_all = h_ref[...].astype(F32)
    for b in range(basis):
        acc = jnp.zeros((2 * LANES, LANES), F32)
        for t in range(taps):
            acc = jnp.where(tap == t, h_all[b : b + 1, t : t + 1], acc)
        toep_ref[:, b * LANES : (b + 1) * LANES] = acc.astype(BF16)

    span = basis * RB
    repeat = (iota((basis, span), 1) // RB == iota((basis, span), 0)).astype(F32)
    g_wide = jnp.dot(g_ref[...].astype(F32).T, repeat, precision=HIGH)
    place = iota((OR, span), 0)
    out_row = jnp.where(place < RB + margin, place, place - OR)
    tap = iota((OR, span), 1) % RB - out_row + margin
    valid = (place < RB + margin) | (place >= OR - margin)
    g_taps = jnp.zeros((OR, span), F32)
    for t in range(taps):
        g_taps = jnp.where(tap == t, g_wide[t : t + 1, :], g_taps)
    g_taps = jnp.where(valid, g_taps, 0.0)
    y = ((band * RB + out_row).astype(F32) + 0.5) * (2.0 / (RB * lax.axis_size("band"))) - 1.0
    for n in range(NB):
        table = coef_ref[ids_ref[0, n]]
        c = jnp.dot(table.T, repeat, precision=HIGH)
        in_x = [
            c[0:1] + c[2:3] * y + c[5:6] * (y * y),
            c[1:2] + c[4:5] * y,
            c[3:4] + jnp.zeros_like(y),
        ]
        for k in range(3):
            rows_ref[n, k * OR : (k + 1) * OR, :] = (g_taps * in_x[k]).astype(BF16)

    cover = cover_ref[...].astype(F32)
    mine = jnp.where(iota(cover.shape, 0) == visit, cover, 0.0)
    weight = weight_ref[...]
    dims = (((0,), (0,)), ((), ()))
    denom = lax.dot_general(cover, weight, dims, precision=HIGH)
    own = lax.dot_general(mine, weight, dims, precision=HIGH)
    factor = own / denom
    for n in range(NB):
        scale_ref[n] = jnp.broadcast_to(factor[:, n : n + 1], (visits, LANES))

    def group_step(rel_z, _):
        z = (my_z + rel_z) % ZN
        first = pl.multiple_of(z * GW, GW)
        lhs = jnp.concatenate(
            [shifted_ref[:, pl.ds(first + k * LANES, 2 * LANES)] for k in range(GROUP)], axis=0
        )
        for pair in range(basis // 2):
            res = mm(lhs, toep_ref[:, pair * 2 * LANES : (pair + 1) * 2 * LANES]).astype(BF16)
            for k in range(GROUP):
                for n in range(NB):
                    for b in range(2):
                        across_ref[
                            n,
                            (2 * pair + b) * RB : (2 * pair + b + 1) * RB,
                            k * LANES : (k + 1) * LANES,
                        ] = res[
                            (k * NB + n) * RB : (k * NB + n + 1) * RB,
                            b * LANES : (b + 1) * LANES,
                        ]
        for x in range(XN):
            lanes = slice(x * 2 * LANES, (x + 1) * 2 * LANES)
            col = (first + x * 2 * LANES + iota((1, 2 * LANES), 1)).astype(F32)
            xc = (col + 0.5) * (2.0 / width) - 1.0
            patch = z * GROUP + x * CN
            parts = []
            for n in range(NB):
                res = mm(rows_ref[n], across_ref[n, :, lanes])
                total = res[:OR] + xc * (res[OR : 2 * OR] + xc * res[2 * OR :])
                scale = jnp.concatenate(
                    [scale_ref[n, pl.ds(patch + c, 1), :] for c in range(CN)], axis=1
                )
                parts.append(total * scale)
            full = jnp.concatenate(
                [parts[0][:RB], parts[1][:RB], parts[0][RB:], parts[1][RB:]], axis=0
            )
            even, odd = full[:, :LANES], full[:, LANES:]
            slot = my_x ^ x
            keep_ref[rel_z, slot] = jnp.where(core == 0, even, odd).astype(BF16)
            send_ref[rel_z, slot] = jnp.where(core == 0, odd, even).astype(BF16)
        return 0

    lax.fori_loop(0, ZN, group_step, 0)


def ring(step):
    return [(i, step(i // GROUP, (i // CN) % XN, i % CN)) for i in range(ZN * GROUP)]


def at(z, x, c):
    return (z % ZN) * GROUP + x * CN + c


SIBLING = ring(lambda z, x, c: at(z, x, c ^ 1))
X_A = ring(lambda z, x, c: at(z, x ^ 1, c))
X_B = ring(lambda z, x, c: at(z, x ^ 3, c))
Z_UP = ring(lambda z, x, c: at(z + 1, x, c))
Z_DOWN = ring(lambda z, x, c: at(z - 1, x, c))


def final_kernel(own_ref, up_ref, down_ref, above_ref, below_ref, out_ref):
    total = own_ref[...] + up_ref[...] + down_ref[...]
    lanes = total.shape[1]
    row = iota((16, lanes), 0)
    for n in range(NB):
        rows = total[n * RB : (n + 1) * RB]
        over = above_ref[n * HALO : n * HALO + 16]
        under = below_ref[n * HALO + 8 : (n + 1) * HALO]
        out_ref[n, :16] = rows[:16] + jnp.where(row < 10, over, 0.0)
        out_ref[n, 16:] = rows[16:] + jnp.where(row >= 6, under, 0.0)


def local(
    source,
    row_start,
    row_weight,
    col_start,
    col_weight,
    col_offset,
    g_taps,
    h_taps,
    coef_table,
    table_ids,
    vis_weight,
    coverage,
):
    vmem = pl.BlockSpec(memory_space=pltpu.VMEM)
    smem = pl.BlockSpec(memory_space=pltpu.SMEM)
    basis = g_taps.shape[0]
    width = col_start.shape[1]
    half = jax.ShapeDtypeStruct((ZN, XN, PR, LANES), BF16)
    keep, send = pl.pallas_call(
        compute_kernel,
        out_shape=(half, half),
        in_specs=[smem, smem] + [vmem] * 10,
        out_specs=(vmem, vmem),
        scratch_shapes=[
            pltpu.VMEM((NB * RB, source.shape[3]), BF16),
            pltpu.VMEM((NB * RB, width + LANES), BF16),
            pltpu.VMEM((2 * LANES, basis * LANES), BF16),
            pltpu.VMEM((NB, 3 * OR, basis * RB), BF16),
            pltpu.VMEM((NB, coverage.shape[1], LANES), F32),
            pltpu.VMEM((NB, basis * RB, GW), BF16),
        ],
        compiler_params=pltpu.CompilerParams(vmem_limit_bytes=40 * 1024 * 1024),
    )(
        col_offset,
        table_ids,
        source,
        row_start,
        row_weight,
        col_start,
        col_weight,
        g_taps,
        h_taps,
        coef_table,
        vis_weight,
        coverage,
    )

    got = lax.ppermute(send, "visit", SIBLING)
    both = keep.astype(F32) + got.astype(F32)
    first, second = both[: ZN // 2], both[ZN // 2 :]
    send_a = jnp.stack([first[:, 1], first[:, 2]]).astype(BF16)
    send_b = jnp.stack([second[:, 3], second[:, 2]]).astype(BF16)
    got_a = lax.ppermute(send_a, "visit", X_A).astype(F32)
    got_b = lax.ppermute(send_b, "visit", X_B).astype(F32)
    send_2b = (first[:, 3] + got_a[1]).astype(BF16)
    send_2a = (second[:, 1] + got_b[1]).astype(BF16)
    got_2b = lax.ppermute(send_2b, "visit", X_B).astype(F32)
    got_2a = lax.ppermute(send_2a, "visit", X_A).astype(F32)
    plane = jnp.concatenate(
        [first[:, 0] + got_a[0] + got_2b, second[:, 0] + got_b[0] + got_2a], axis=0
    )

    up = lax.ppermute(plane[4], "visit", Z_UP)
    up = lax.ppermute(plane[3] + up, "visit", Z_UP)
    down = lax.ppermute(plane[5], "visit", Z_DOWN)
    up = lax.ppermute(plane[2] + up, "visit", Z_UP)
    down = lax.ppermute(plane[6] + down, "visit", Z_DOWN)
    up = lax.ppermute(plane[1] + up, "visit", Z_UP)
    down = lax.ppermute(plane[7] + down, "visit", Z_DOWN)
    own = plane[0]

    halo = own[NB * RB :] + up[NB * RB :] + down[NB * RB :]
    count = lax.axis_size("band")
    above = lax.ppermute(halo, "band", [(i, i + 1) for i in range(count - 1)])
    below = lax.ppermute(halo, "band", [(i + 1, i) for i in range(count - 1)])
    return pl.pallas_call(
        final_kernel,
        out_shape=jax.ShapeDtypeStruct((NB, RB, LANES), F32),
        in_specs=[vmem] * 5,
        out_specs=vmem,
    )(own[: NB * RB], up[: NB * RB], down[: NB * RB], above, below)


def solution(mesh):
    in_specs = (
        P("visit", None, "band", None),
        P("visit", "band"),
        P("visit", None, "band"),
        P("visit", None),
        P("visit", None, None),
        P("visit", None),
        P(),
        P(),
        P(),
        P("visit", None),
        P(),
        P(),
    )
    out_specs = P(None, "band", "visit")
    return jax.shard_map(local, mesh=mesh, in_specs=in_specs, out_specs=out_specs, check_vma=False)
```

```python
import jax
import jax.numpy as jnp
from jax import lax
from jax.sharding import PartitionSpec as P
from jax.experimental import pallas as pl
from jax.experimental.pallas import tpu as pltpu

F32 = jnp.float32
BF16 = jnp.bfloat16
HIGH = lax.Precision.HIGHEST

NB = 2
RB = 32
SR = 40
LANES = 128
ZN, XN, CN = 8, 4, 2
GROUP = XN * CN
GW = GROUP * LANES
HALO = 24
OR = RB + HALO
PR = NB * OR
HALF = LANES // 2


def iota(shape, dim):
    return lax.broadcasted_iota(jnp.int32, shape, dim)


def mm(a, b):
    return jnp.dot(a, b, preferred_element_type=F32)


def compute_kernel(
    off_hbm,
    ids_hbm,
    source_hbm,
    row_start_hbm,
    row_weight_hbm,
    col_start_hbm,
    col_weight_hbm,
    g_hbm,
    h_hbm,
    coef_hbm,
    weight_hbm,
    cover_hbm,
    keep_ref,
    send_ref,
    off_ref,
    ids_ref,
    source_ref,
    row_start_ref,
    row_weight_ref,
    col_start_ref,
    col_weight_ref,
    g_ref,
    h_ref,
    coef_ref,
    weight_ref,
    cover_ref,
    rowres_ref,
    shifted_ref,
    toep_ref,
    rows_ref,
    scale_ref,
    across_ref,
    sems,
):
    pairs = [
        (h_hbm, h_ref),
        (g_hbm, g_ref),
        (coef_hbm, coef_ref),
        (ids_hbm, ids_ref),
        (weight_hbm, weight_ref),
        (cover_hbm, cover_ref),
        (row_start_hbm, row_start_ref),
        (row_weight_hbm, row_weight_ref),
        (source_hbm, source_ref),
        (off_hbm, off_ref),
        (col_start_hbm, col_start_ref),
        (col_weight_hbm, col_weight_ref),
    ]
    copies = [pltpu.make_async_copy(a, b, sems.at[i]) for i, (a, b) in enumerate(pairs)]
    for copy in copies:
        copy.start()
    visit = lax.axis_index("visit")
    band = lax.axis_index("band")
    core = visit % CN
    my_x = (visit // CN) % XN
    taps = g_ref.shape[1]
    margin = taps // 2
    basis = g_ref.shape[0]
    blocks = off_ref.shape[1]
    width = blocks * LANES
    visits = cover_ref.shape[0]

    for copy in copies[:6]:
        copy.wait()

    tap = iota((2 * LANES, LANES), 0) - iota((2 * LANES, LANES), 1) - (HALF - margin)
    h_all = h_ref[...].astype(F32)
    for b in range(basis):
        acc = jnp.zeros((2 * LANES, LANES), F32)
        for t in range(taps):
            acc = jnp.where(tap == t, h_all[b : b + 1, t : t + 1], acc)
        toep_ref[:, b * LANES : (b + 1) * LANES] = acc.astype(BF16)

    span = basis * RB
    repeat = (iota((basis, span), 1) // RB == iota((basis, span), 0)).astype(F32)
    g_wide = jnp.dot(g_ref[...].astype(F32).T, repeat, precision=HIGH)
    place = iota((OR, span), 0)
    out_row = jnp.where(place < RB + margin, place, place - OR)
    tap = iota((OR, span), 1) % RB - out_row + margin
    valid = (place < RB + margin) | (place >= OR - margin)
    g_taps = jnp.zeros((OR, span), F32)
    for t in range(taps):
        g_taps = jnp.where(tap == t, g_wide[t : t + 1, :], g_taps)
    g_taps = jnp.where(valid, g_taps, 0.0)
    y = ((band * RB + out_row).astype(F32) + 0.5) * (2.0 / (RB * lax.axis_size("band"))) - 1.0
    for n in range(NB):
        table = coef_ref[:, pl.ds(ids_ref[0, n], 1), :].reshape(coef_ref.shape[0], basis)
        c = jnp.dot(table, repeat, precision=HIGH)
        in_x = [
            c[0:1] + c[2:3] * y + c[5:6] * (y * y),
            c[1:2] + c[4:5] * y,
            c[3:4] + jnp.zeros_like(y),
        ]
        for k in range(3):
            rows_ref[n, k * OR : (k + 1) * OR, :] = (g_taps * in_x[k]).astype(BF16)

    cover = cover_ref[...].astype(F32)
    mine = jnp.where(iota(cover.shape, 0) == visit, cover, 0.0)
    weight = weight_ref[...]
    dims = (((0,), (1,)), ((), ()))
    denom = lax.dot_general(cover, weight, dims, precision=HIGH)
    own = lax.dot_general(mine, weight, dims, precision=HIGH)
    factor = own / denom
    for n in range(NB):
        scale_ref[n] = jnp.broadcast_to(factor[:, n : n + 1], (visits, LANES))

    for copy in copies[6:]:
        copy.wait()

    start = row_start_ref[...]
    weights = row_weight_ref[0].astype(F32)
    rel = iota((SR, RB), 0) - start
    picked = jnp.zeros((SR, RB), F32)
    for q in range(4):
        picked = jnp.where(rel == q, weights[q : q + 1, :], picked)
    picker = picked.T.astype(BF16)
    chunk = 2 * LANES

    def row_step(j, _):
        cols = pl.ds(pl.multiple_of(j * chunk, chunk), chunk)
        for n in range(NB):
            rowres_ref[n * RB : (n + 1) * RB, cols] = mm(
                picker, source_ref[0, n, :, cols]
            ).astype(BF16)
        return 0

    lax.fori_loop(0, rowres_ref.shape[1] // chunk, row_step, 0, unroll=3)

    low = iota((NB * RB, LANES), 1) < HALF
    tall = 3 * LANES
    tall_iota = iota((tall, LANES), 0)

    def col_step(c, before):
        first = pl.multiple_of(c * LANES, LANES)
        cols = pl.ds(first, LANES)
        at = col_start_ref[0:1, cols] + off_ref[0, c]
        wts = col_weight_ref[0, :, cols].astype(F32)
        rel = tall_iota - at
        spread = jnp.zeros((tall, LANES), F32)
        for q in range(4):
            spread = jnp.where(rel == q, wts[q : q + 1, :], spread)
        res = mm(rowres_ref[:, pl.ds(first, tall)], spread.astype(BF16))
        rolled = pltpu.roll(res, HALF, 1)
        shifted_ref[:, cols] = jnp.where(low, before, rolled).astype(BF16)
        return rolled

    last = lax.fori_loop(0, blocks, col_step, jnp.zeros((NB * RB, LANES), F32), unroll=4)
    shifted_ref[:, width : width + LANES] = jnp.where(low, last, 0.0).astype(BF16)

    def group_step(z, _):
        first = pl.multiple_of(z * GW, GW)
        lhs = jnp.concatenate(
            [shifted_ref[:, pl.ds(first + k * LANES, 2 * LANES)] for k in range(GROUP)], axis=0
        )
        for pair in range(basis // 2):
            res = mm(lhs, toep_ref[:, pair * 2 * LANES : (pair + 1) * 2 * LANES]).astype(BF16)
            for k in range(GROUP):
                for n in range(NB):
                    for b in range(2):
                        across_ref[
                            n,
                            (2 * pair + b) * RB : (2 * pair + b + 1) * RB,
                            k * LANES : (k + 1) * LANES,
                        ] = res[
                            (k * NB + n) * RB : (k * NB + n + 1) * RB,
                            b * LANES : (b + 1) * LANES,
                        ]
        for x in range(XN):
            lanes = slice(x * 2 * LANES, (x + 1) * 2 * LANES)
            col = (first + x * 2 * LANES + iota((1, 2 * LANES), 1)).astype(F32)
            xc = (col + 0.5) * (2.0 / width) - 1.0
            patch = z * GROUP + x * CN
            parts = []
            for n in range(NB):
                res = mm(rows_ref[n], across_ref[n, :, lanes])
                total = res[:OR] + xc * (res[OR : 2 * OR] + xc * res[2 * OR :])
                scale = jnp.concatenate(
                    [scale_ref[n, pl.ds(patch + c, 1), :] for c in range(CN)], axis=1
                )
                parts.append(total * scale)
            full = jnp.concatenate(
                [parts[0][:RB], parts[1][:RB], parts[0][RB:], parts[1][RB:]], axis=0
            )
            even, odd = full[:, :LANES], full[:, LANES:]
            slot = my_x ^ x
            keep_ref[slot, z] = jnp.where(core == 0, even, odd)
            send_ref[slot, z] = jnp.where(core == 0, odd, even).astype(BF16)
        return 0

    lax.fori_loop(0, ZN, group_step, 0)


def ring(step):
    return [(i, step(i // GROUP, (i // CN) % XN, i % CN)) for i in range(ZN * GROUP)]


def at(z, x, c):
    return (z % ZN) * GROUP + x * CN + c


SIBLING = ring(lambda z, x, c: at(z, x, c ^ 1))
ACROSS_X = [ring(lambda z, x, c, d=d: at(z, x ^ d, c)) for d in range(1, XN)]
ALONG_Z = [[at(z, x, c) for z in range(ZN)] for x in range(XN) for c in range(CN)]


def local(
    source,
    row_start,
    row_weight,
    col_start,
    col_weight,
    col_offset,
    g_taps,
    h_taps,
    coef_table,
    table_ids,
    vis_weight,
    coverage,
):
    basis = g_taps.shape[0]
    width = col_start.shape[1]
    operands = (
        col_offset,
        table_ids,
        source,
        row_start,
        row_weight,
        col_start,
        col_weight,
        g_taps,
        h_taps,
        coef_table.transpose(2, 0, 1),
        vis_weight.T,
        coverage,
    )
    vmem = pl.BlockSpec(memory_space=pltpu.VMEM)
    local_copies = [
        (pltpu.SMEM if k < 2 else pltpu.VMEM)(a.shape, a.dtype) for k, a in enumerate(operands)
    ]
    keep, send = pl.pallas_call(
        compute_kernel,
        out_shape=(
            jax.ShapeDtypeStruct((XN, ZN, PR, LANES), F32),
            jax.ShapeDtypeStruct((XN, ZN, PR, LANES), BF16),
        ),
        in_specs=[pl.BlockSpec(memory_space=pltpu.HBM)] * len(operands),
        out_specs=(vmem, vmem),
        scratch_shapes=local_copies
        + [
            pltpu.VMEM((NB * RB, source.shape[3]), BF16),
            pltpu.VMEM((NB * RB, width + LANES), BF16),
            pltpu.VMEM((2 * LANES, basis * LANES), BF16),
            pltpu.VMEM((NB, 3 * OR, basis * RB), BF16),
            pltpu.VMEM((NB, coverage.shape[1], LANES), F32),
            pltpu.VMEM((NB, basis * RB, GW), BF16),
            pltpu.SemaphoreType.DMA((len(operands),)),
        ],
        compiler_params=pltpu.CompilerParams(vmem_limit_bytes=40 * 1024 * 1024),
    )(*operands)

    got = lax.ppermute(send, "visit", SIBLING)
    both = keep + got.astype(F32)
    from_x = [
        lax.ppermute(both[d].astype(BF16), "visit", ACROSS_X[d - 1]) for d in range(1, XN)
    ]
    plane = both[0] + sum(part.astype(F32) for part in from_x)
    from_z = lax.all_to_all(
        plane.astype(BF16), "visit", 0, 0, axis_index_groups=ALONG_Z, tiled=True
    )

    halo = jnp.sum(from_z[:, NB * RB :].astype(F32), axis=0)
    count = lax.axis_size("band")
    band = lax.axis_index("band")
    above = lax.ppermute(halo, "band", [(i, (i + 1) % count) for i in range(count)])
    below = lax.ppermute(halo, "band", [((i + 1) % count, i) for i in range(count)])
    own = jnp.sum(from_z[:, : NB * RB].astype(F32), axis=0).reshape(NB, RB, LANES)
    above = above.reshape(NB, HALO, LANES)[:, :10]
    below = below.reshape(NB, HALO, LANES)[:, HALO - 10 :]
    above = jnp.pad(above, ((0, 0), (0, RB - 10), (0, 0)))
    below = jnp.pad(below, ((0, 0), (RB - 10, 0), (0, 0)))
    return own + jnp.where(band > 0, above, 0.0) + jnp.where(band < count - 1, below, 0.0)


def solution(mesh):
    in_specs = (
        P("visit", None, "band", None),
        P("visit", "band"),
        P("visit", None, "band"),
        P("visit", None),
        P("visit", None, None),
        P("visit", None),
        P(),
        P(),
        P(),
        P("visit", None),
        P(),
        P(),
    )
    out_specs = P(None, "band", "visit")
    return jax.shard_map(local, mesh=mesh, in_specs=in_specs, out_specs=out_specs, check_vma=False)
```

```python
import jax
import jax.numpy as jnp
from jax import lax
from jax.sharding import PartitionSpec as P
from jax.experimental import pallas as pl
from jax.experimental.pallas import tpu as pltpu

F32 = jnp.float32
I16 = jnp.int16
BF16 = jnp.bfloat16
HIGH = lax.Precision.HIGHEST

NB = 2
RB = 32
SR = 40
LANES = 128
ZN, XN, CN = 8, 4, 2
GROUP = XN * CN
GW = GROUP * LANES
HALO = 24
OR = RB + HALO
PR = NB * OR
HALF = LANES // 2


def iota(shape, dim):
    return lax.broadcasted_iota(jnp.int32, shape, dim)


def mm(a, b):
    return jnp.dot(a, b, preferred_element_type=F32)


def filter_groups(
    first_z, keep_ref, send_ref, shifted_ref, toep_ref, rows_ref, scale_ref, across_ref
):
    visit = lax.axis_index("visit")
    core = visit % CN
    my_x = (visit // CN) % XN
    basis = toep_ref.shape[1] // LANES
    width = shifted_ref.shape[1] - LANES

    def group_step(place, _):
        z = place + first_z
        first = pl.multiple_of(z * GW, GW)
        lhs = jnp.concatenate(
            [shifted_ref[:, pl.ds(first + k * LANES, 2 * LANES)] for k in range(GROUP)], axis=0
        )
        for pair in range(basis // 2):
            res = mm(lhs, toep_ref[:, pair * 2 * LANES : (pair + 1) * 2 * LANES]).astype(BF16)
            for k in range(GROUP):
                for n in range(NB):
                    for b in range(2):
                        across_ref[
                            n,
                            (2 * pair + b) * RB : (2 * pair + b + 1) * RB,
                            k * LANES : (k + 1) * LANES,
                        ] = res[
                            (k * NB + n) * RB : (k * NB + n + 1) * RB,
                            b * LANES : (b + 1) * LANES,
                        ]
        for x in range(XN):
            lanes = slice(x * 2 * LANES, (x + 1) * 2 * LANES)
            col = (first + x * 2 * LANES + iota((1, 2 * LANES), 1)).astype(F32)
            xc = (col + 0.5) * (2.0 / width) - 1.0
            patch = z * GROUP + x * CN
            parts = []
            for n in range(NB):
                res = mm(rows_ref[n], across_ref[n, :, lanes])
                total = res[:OR] + xc * (res[OR : 2 * OR] + xc * res[2 * OR :])
                scale = jnp.concatenate(
                    [scale_ref[n, pl.ds(patch + c, 1), :] for c in range(CN)], axis=1
                )
                parts.append(total * scale)
            full = jnp.concatenate(
                [parts[0][:RB], parts[1][:RB], parts[0][RB:], parts[1][RB:]], axis=0
            )
            even, odd = full[:, :LANES], full[:, LANES:]
            slot = my_x ^ x
            keep_ref[slot, place] = jnp.where(core == 0, even, odd)
            send_ref[slot, place] = jnp.where(core == 0, odd, even).astype(BF16)
        return 0

    lax.fori_loop(0, keep_ref.shape[1], group_step, 0, unroll=2)


def compute_kernel(
    off_hbm,
    ids_hbm,
    source_hbm,
    row_start_hbm,
    row_weight_hbm,
    col_start_hbm,
    col_weight_hbm,
    g_hbm,
    h_hbm,
    coef_hbm,
    weight_hbm,
    cover_hbm,
    keep_ref,
    send_ref,
    off_ref,
    ids_ref,
    source_ref,
    row_start_ref,
    row_weight_ref,
    col_start_ref,
    col_weight_ref,
    g_ref,
    h_ref,
    coef_ref,
    weight_ref,
    cover_ref,
    rowres_ref,
    shifted_ref,
    toep_ref,
    rows_ref,
    scale_ref,
    across_ref,
    sems,
):
    pairs = [
        (h_hbm, h_ref),
        (g_hbm, g_ref),
        (coef_hbm, coef_ref),
        (ids_hbm, ids_ref),
        (weight_hbm, weight_ref),
        (cover_hbm, cover_ref),
        (row_start_hbm, row_start_ref),
        (row_weight_hbm, row_weight_ref),
        (source_hbm, source_ref),
        (off_hbm, off_ref),
        (col_start_hbm, col_start_ref),
        (col_weight_hbm, col_weight_ref),
    ]
    copies = [pltpu.make_async_copy(a, b, sems.at[i]) for i, (a, b) in enumerate(pairs)]
    for copy in copies:
        copy.start()
    visit = lax.axis_index("visit")
    band = lax.axis_index("band")
    taps = g_ref.shape[1]
    margin = taps // 2
    basis = g_ref.shape[0]
    blocks = off_ref.shape[1]
    width = blocks * LANES
    visits = cover_ref.shape[0]

    for copy in copies[:6]:
        copy.wait()

    tile = (2 * LANES, LANES)
    tap = (iota(tile, 0) - iota(tile, 1) - (HALF - margin)).astype(I16)
    h_all = h_ref[...].astype(F32)
    for b in range(basis):
        acc = jnp.zeros(tile, BF16)
        for t in range(taps):
            acc = jnp.where(
                tap == t, jnp.broadcast_to(h_all[b : b + 1, t : t + 1], tile).astype(BF16), acc
            )
        toep_ref[:, b * LANES : (b + 1) * LANES] = acc

    span = basis * RB
    repeat = (iota((basis, span), 1) // RB == iota((basis, span), 0)).astype(F32)
    g_wide = mm(g_ref[...].astype(F32).T.astype(BF16), repeat.astype(BF16))
    place = iota((OR, span), 0)
    out_row = jnp.where(place < RB + margin, place, place - OR)
    tap = iota((OR, span), 1) % RB - out_row + margin
    tract_row = band * RB + out_row
    valid = (place < RB + margin) | (place >= OR - margin)
    valid &= (tract_row >= 0) & (tract_row < RB * lax.axis_size("band"))
    g_taps = jnp.zeros((OR, span), F32)
    for t in range(taps):
        g_taps = jnp.where(tap == t, g_wide[t : t + 1, :], g_taps)
    g_taps = jnp.where(valid, g_taps, 0.0)
    y = (tract_row.astype(F32) + 0.5) * (2.0 / (RB * lax.axis_size("band"))) - 1.0
    for n in range(NB):
        table = coef_ref[:, pl.ds(ids_ref[0, n], 1), :].reshape(coef_ref.shape[0], basis)
        c = jnp.dot(table, repeat, precision=HIGH)
        in_x = [
            c[0:1] + c[2:3] * y + c[5:6] * (y * y),
            c[1:2] + c[4:5] * y,
            c[3:4] + jnp.zeros_like(y),
        ]
        for k in range(3):
            rows_ref[n, k * OR : (k + 1) * OR, :] = (g_taps * in_x[k]).astype(BF16)

    cover = cover_ref[...].astype(F32)
    mine = jnp.where(iota(cover.shape, 0) == visit, cover, 0.0)
    weight = weight_ref[...]
    dims = (((0,), (1,)), ((), ()))
    denom = lax.dot_general(cover, weight, dims, precision=HIGH)
    own = lax.dot_general(mine, weight, dims, precision=HIGH)
    factor = own / denom
    for n in range(NB):
        scale_ref[n] = jnp.broadcast_to(factor[:, n : n + 1], (visits, LANES))

    for copy in copies[6:]:
        copy.wait()

    start = row_start_ref[...]
    weights = row_weight_ref[0].astype(F32)
    rel = iota((SR, RB), 0) - start
    picked = jnp.zeros((SR, RB), F32)
    for q in range(4):
        picked = jnp.where(rel == q, weights[q : q + 1, :], picked)
    picker = picked.T.astype(BF16)
    chunk = 2 * LANES

    def row_step(j, _):
        cols = pl.ds(pl.multiple_of(j * chunk, chunk), chunk)
        for n in range(NB):
            rowres_ref[n * RB : (n + 1) * RB, cols] = mm(
                picker, source_ref[0, n, :, cols]
            ).astype(BF16)
        return 0

    lax.fori_loop(0, rowres_ref.shape[1] // chunk, row_step, 0, unroll=11)

    low = iota((NB * RB, LANES), 1) < HALF
    tall = 3 * LANES
    tall_iota = iota((tall, LANES), 0).astype(I16)

    def col_step(c, before):
        first = pl.multiple_of(c * LANES, LANES)
        cols = pl.ds(first, LANES)
        at = col_start_ref[0:1, cols] + off_ref[0, c]
        wts = col_weight_ref[0, :, cols]
        rel = tall_iota - jnp.broadcast_to(at, (tall, LANES)).astype(I16)
        spread = jnp.zeros((tall, LANES), BF16)
        for q in range(4):
            spread = jnp.where(rel == q, jnp.broadcast_to(wts[q : q + 1, :], (tall, LANES)), spread)
        res = mm(rowres_ref[:, pl.ds(first, tall)], spread)
        rolled = pltpu.roll(res, HALF, 1)
        shifted_ref[:, cols] = jnp.where(low, before, rolled).astype(BF16)
        return rolled

    last = lax.fori_loop(0, blocks, col_step, jnp.zeros((NB * RB, LANES), F32), unroll=16)
    shifted_ref[:, width : width + LANES] = jnp.where(low, last, 0.0).astype(BF16)

    filter_groups(
        0, keep_ref, send_ref, shifted_ref, toep_ref, rows_ref, scale_ref, across_ref
    )


def ring(step):
    return [(i, step(i // GROUP, (i // CN) % XN, i % CN)) for i in range(ZN * GROUP)]


def at(z, x, c):
    return (z % ZN) * GROUP + x * CN + c


SIBLING = ring(lambda z, x, c: at(z, x, c ^ 1))
ACROSS_X = [ring(lambda z, x, c, d=d: at(z, x ^ d, c)) for d in range(1, XN)]
ALONG_Z = [[at(z, x, c) for z in range(ZN)] for x in range(XN) for c in range(CN)]


def exchange_core(keep, send):
    both = keep + lax.ppermute(send, "visit", SIBLING).astype(F32)
    return both[0], [both[d].astype(BF16) for d in range(1, XN)]


def exchange_x(own, sends):
    got = [lax.ppermute(part, "visit", to) for part, to in zip(sends, ACROSS_X)]
    return (own + sum(part.astype(F32) for part in got)).astype(BF16)


def local(
    source,
    row_start,
    row_weight,
    col_start,
    col_weight,
    col_offset,
    g_taps,
    h_taps,
    coef_table,
    table_ids,
    vis_weight,
    coverage,
):
    basis = g_taps.shape[0]
    width = col_start.shape[1]
    operands = (
        col_offset,
        table_ids,
        source,
        row_start,
        row_weight,
        col_start,
        col_weight,
        g_taps,
        h_taps,
        coef_table.transpose(2, 0, 1),
        vis_weight.T,
        coverage,
    )
    vmem = pl.BlockSpec(memory_space=pltpu.VMEM)
    local_copies = [
        (pltpu.SMEM if k < 2 else pltpu.VMEM)(a.shape, a.dtype) for k, a in enumerate(operands)
    ]
    limit = pltpu.CompilerParams(vmem_limit_bytes=20 * 1024 * 1024)
    partial = (
        jax.ShapeDtypeStruct((XN, ZN, PR, LANES), F32),
        jax.ShapeDtypeStruct((XN, ZN, PR, LANES), BF16),
    )
    across = pltpu.VMEM((NB, basis * RB, GW), BF16)
    keep, send = pl.pallas_call(
        compute_kernel,
        out_shape=partial,
        in_specs=[pl.BlockSpec(memory_space=pltpu.HBM)] * len(operands),
        out_specs=(vmem,) * 2,
        scratch_shapes=local_copies
        + [
            pltpu.VMEM((NB * RB, source.shape[3]), BF16),
            pltpu.VMEM((NB * RB, width + LANES), BF16),
            pltpu.VMEM((2 * LANES, basis * LANES), BF16),
            pltpu.VMEM((NB, 3 * OR, basis * RB), BF16),
            pltpu.VMEM((NB, coverage.shape[1], LANES), F32),
            across,
            pltpu.SemaphoreType.DMA((len(operands),)),
        ],
        compiler_params=limit,
    )(*(pltpu.with_memory_space_constraint(a, pltpu.HBM) for a in operands))

    plane = exchange_x(*exchange_core(keep, send))
    from_z = lax.all_to_all(
        plane, "visit", 0, 0, axis_index_groups=ALONG_Z, tiled=True
    )

    halo = jnp.sum(from_z[:, NB * RB :].astype(F32), axis=0)
    count = lax.axis_size("band")
    above = lax.ppermute(halo, "band", [(i, (i + 1) % count) for i in range(count)])
    below = lax.ppermute(halo, "band", [((i + 1) % count, i) for i in range(count)])
    own = jnp.sum(from_z[:, : NB * RB].astype(F32), axis=0).reshape(NB, RB, LANES)
    above = above.reshape(NB, HALO, LANES)[:, :10]
    below = below.reshape(NB, HALO, LANES)[:, HALO - 10 :]
    above = jnp.pad(above, ((0, 0), (0, RB - 10), (0, 0)))
    below = jnp.pad(below, ((0, 0), (RB - 10, 0), (0, 0)))
    return own + above + below


def solution(mesh):
    in_specs = (
        P("visit", None, "band", None),
        P("visit", "band"),
        P("visit", None, "band"),
        P("visit", None),
        P("visit", None, None),
        P("visit", None),
        P(),
        P(),
        P(),
        P("visit", None),
        P(),
        P(),
    )
    out_specs = P(None, "band", "visit")
    return jax.shard_map(local, mesh=mesh, in_specs=in_specs, out_specs=out_specs, check_vma=False)
```

```python
import jax
import jax.numpy as jnp
from jax import lax
from jax.sharding import PartitionSpec as P
from jax.experimental import pallas as pl
from jax.experimental.pallas import tpu as pltpu

F32 = jnp.float32
I16 = jnp.int16
BF16 = jnp.bfloat16
HIGH = lax.Precision.HIGHEST

NB = 2
RB = 32
SR = 40
LANES = 128
ZN, XN, CN = 8, 4, 2
GROUP = XN * CN
GW = GROUP * LANES
EDGE = 16
OR = RB + 2 * EDGE
HALF = LANES // 2


def iota(shape, dim):
    return lax.broadcasted_iota(jnp.int32, shape, dim)


def mm(a, b):
    return jnp.dot(a, b, preferred_element_type=F32)


def compute_kernel(
    off_hbm,
    ids_hbm,
    source_hbm,
    row_start_hbm,
    row_weight_hbm,
    col_start_hbm,
    col_weight_hbm,
    g_hbm,
    h_hbm,
    coef_hbm,
    weight_hbm,
    cover_hbm,
    keep_ref,
    send_ref,
    off_ref,
    ids_ref,
    source_ref,
    row_start_ref,
    row_weight_ref,
    col_start_ref,
    col_weight_ref,
    g_ref,
    h_ref,
    coef_ref,
    weight_ref,
    cover_ref,
    rowres_ref,
    shifted_ref,
    toep_ref,
    rows_ref,
    scale_ref,
    across_ref,
    sems,
):
    pairs = [
        (h_hbm, h_ref),
        (g_hbm, g_ref),
        (coef_hbm, coef_ref),
        (ids_hbm, ids_ref),
        (weight_hbm, weight_ref),
        (cover_hbm, cover_ref),
        (row_start_hbm, row_start_ref),
        (row_weight_hbm, row_weight_ref),
        (source_hbm, source_ref),
        (off_hbm, off_ref),
        (col_start_hbm, col_start_ref),
        (col_weight_hbm, col_weight_ref),
    ]
    copies = [pltpu.make_async_copy(a, b, sems.at[i]) for i, (a, b) in enumerate(pairs)]
    for copy in copies:
        copy.start()
    visit = lax.axis_index("visit")
    band = lax.axis_index("band")
    taps = g_ref.shape[1]
    margin = taps // 2
    basis = g_ref.shape[0]
    blocks = off_ref.shape[1]
    width = blocks * LANES
    visits = cover_ref.shape[0]

    for copy in copies[:6]:
        copy.wait()

    tile = (2 * LANES, LANES)
    tap = (iota(tile, 0) - iota(tile, 1) - (HALF - margin)).astype(I16)
    h_all = h_ref[...].astype(F32)
    for b in range(basis):
        acc = jnp.zeros(tile, BF16)
        for t in range(taps):
            acc = jnp.where(
                tap == t, jnp.broadcast_to(h_all[b : b + 1, t : t + 1], tile).astype(BF16), acc
            )
        toep_ref[:, b * LANES : (b + 1) * LANES] = acc

    span = basis * RB
    repeat = (iota((basis, span), 1) // RB == iota((basis, span), 0)).astype(F32)
    g_wide = mm(g_ref[...].astype(F32).T.astype(BF16), repeat.astype(BF16))
    place = iota((OR, span), 0)
    out_row = jnp.where(place < RB + margin, place, place - OR)
    tap = iota((OR, span), 1) % RB - out_row + margin
    tract_row = band * RB + out_row
    valid = (place < RB + margin) | (place >= OR - margin)
    valid &= (tract_row >= 0) & (tract_row < RB * lax.axis_size("band"))
    g_taps = jnp.zeros((OR, span), F32)
    for t in range(taps):
        g_taps = jnp.where(tap == t, g_wide[t : t + 1, :], g_taps)
    g_taps = jnp.where(valid, g_taps, 0.0)
    y = (tract_row.astype(F32) + 0.5) * (2.0 / (RB * lax.axis_size("band"))) - 1.0
    for n in range(NB):
        table = coef_ref[:, pl.ds(ids_ref[0, n], 1), :].reshape(coef_ref.shape[0], basis)
        c = jnp.dot(table, repeat, precision=HIGH)
        in_x = [
            c[0:1] + c[2:3] * y + c[5:6] * (y * y),
            c[1:2] + c[4:5] * y,
            c[3:4] + jnp.zeros_like(y),
        ]
        for k in range(3):
            rows_ref[n, k * OR : (k + 1) * OR, :] = (g_taps * in_x[k]).astype(BF16)

    cover = cover_ref[...].astype(F32)
    mine = jnp.where(iota(cover.shape, 0) == visit, cover, 0.0)
    weight = weight_ref[...]
    dims = (((0,), (1,)), ((), ()))
    denom = lax.dot_general(cover, weight, dims, precision=HIGH)
    own = lax.dot_general(mine, weight, dims, precision=HIGH)
    factor = own / denom
    for n in range(NB):
        scale_ref[n] = jnp.broadcast_to(factor[:, n : n + 1], (visits, LANES))

    for copy in copies[6:]:
        copy.wait()

    start = row_start_ref[...]
    weights = row_weight_ref[0].astype(F32)
    rel = iota((SR, RB), 0) - start
    picked = jnp.zeros((SR, RB), F32)
    for q in range(4):
        picked = jnp.where(rel == q, weights[q : q + 1, :], picked)
    picker = picked.T.astype(BF16)
    chunk = 2 * LANES

    def row_step(j, _):
        cols = pl.ds(pl.multiple_of(j * chunk, chunk), chunk)
        for n in range(NB):
            rowres_ref[n * RB : (n + 1) * RB, cols] = mm(
                picker, source_ref[0, n, :, cols]
            ).astype(BF16)
        return 0

    lax.fori_loop(0, rowres_ref.shape[1] // chunk, row_step, 0, unroll=11)

    low = iota((NB * RB, 2 * LANES), 1) < HALF
    tall = 3 * LANES
    tall_iota = iota((tall, LANES), 0).astype(I16)

    def col_step(c, before):
        if c == blocks // 2:
            shifted_ref[:, c * 2 * LANES :] = jnp.where(low, before, 0.0).astype(BF16)
            return before
        spreads = []
        for k in range(2):
            cols = slice((2 * c + k) * LANES, (2 * c + k + 1) * LANES)
            at = col_start_ref[0:1, cols] + off_ref[0, 2 * c + k]
            wts = col_weight_ref[0, :, cols]
            rel = tall_iota - jnp.broadcast_to(at, (tall, LANES)).astype(I16)
            spread = jnp.zeros((tall, LANES), BF16)
            for q in range(4):
                spread = jnp.where(
                    rel == q, jnp.broadcast_to(wts[q : q + 1, :], (tall, LANES)), spread
                )
            spreads.append(spread)
        none = jnp.zeros((LANES, LANES), BF16)
        both = jnp.concatenate(
            [
                jnp.concatenate([spreads[0], none], axis=0),
                jnp.concatenate([none, spreads[1]], axis=0),
            ],
            axis=1,
        )
        first = c * 2 * LANES
        res = mm(rowres_ref[:, first : first + tall + LANES], both)
        rolled = pltpu.roll(res, HALF, 1)
        shifted_ref[:, first : first + 2 * LANES] = jnp.where(low, before, rolled).astype(BF16)
        return rolled

    core = visit % CN
    my_x = (visit // CN) % XN

    def window(z):
        return jnp.concatenate(
            [
                shifted_ref[:, (z * GROUP + k) * LANES : (z * GROUP + k + 2) * LANES]
                for k in range(GROUP)
            ],
            axis=0,
        )

    def filter_columns(z, lhs, pair):
        res = mm(lhs, toep_ref[:, pair * 2 * LANES : (pair + 1) * 2 * LANES]).astype(BF16)
        for k in range(GROUP):
            for n in range(NB):
                for b in range(2):
                    across_ref[
                        z % 2,
                        n,
                        (2 * pair + b) * RB : (2 * pair + b + 1) * RB,
                        k * LANES : (k + 1) * LANES,
                    ] = res[
                        (k * NB + n) * RB : (k * NB + n + 1) * RB,
                        b * LANES : (b + 1) * LANES,
                    ]

    def filter_rows(z, x, n):
        col = (z * GW + x * 2 * LANES + iota((1, 2 * LANES), 1)).astype(F32)
        xc = (col + 0.5) * (2.0 / width) - 1.0
        patch = z * GROUP + x * CN
        slot = my_x ^ x
        res = mm(rows_ref[n], across_ref[z % 2, n, :, x * 2 * LANES : (x + 1) * 2 * LANES])
        total = res[:OR] + xc * (res[OR : 2 * OR] + xc * res[2 * OR :])
        scale = jnp.concatenate(
            [scale_ref[n, patch + c : patch + c + 1, :] for c in range(CN)], axis=1
        )
        total = total * scale
        even, odd = total[:, :LANES], total[:, LANES:]
        keep_ref[slot, z, n] = jnp.where(core == 0, even, odd)
        send_ref[slot, z, n] = jnp.where(core == 0, odd, even).astype(BF16)

    before = jnp.zeros((NB * RB, 2 * LANES), F32)
    ready = GROUP // 2 + 1
    for c in range(ready):
        before = col_step(c, before)
    for z in range(ZN + 1):
        lhs = window(z) if z < ZN else None
        for step in range(GROUP):
            if z < ZN:
                filter_columns(z, lhs, step)
            if step % 2 == 0 and ready <= blocks // 2:
                before = col_step(ready, before)
                ready += 1
            if z > 0:
                filter_rows(z - 1, step // 2, step % 2)


def ring(step):
    return [(i, step(i // GROUP, (i // CN) % XN, i % CN)) for i in range(ZN * GROUP)]


def at(z, x, c):
    return (z % ZN) * GROUP + x * CN + c


SIBLING = ring(lambda z, x, c: at(z, x, c ^ 1))
ACROSS_X = [ring(lambda z, x, c, d=d: at(z, x ^ d, c)) for d in range(1, XN)]
ALONG_Z = [[at(z, x, c) for z in range(ZN)] for x in range(XN) for c in range(CN)]


def local(
    source,
    row_start,
    row_weight,
    col_start,
    col_weight,
    col_offset,
    g_taps,
    h_taps,
    coef_table,
    table_ids,
    vis_weight,
    coverage,
):
    basis = g_taps.shape[0]
    width = col_start.shape[1]
    operands = (
        col_offset,
        table_ids,
        source,
        row_start,
        row_weight,
        col_start,
        col_weight,
        g_taps,
        h_taps,
        coef_table.transpose(2, 0, 1),
        vis_weight.T,
        coverage,
    )
    vmem = pl.BlockSpec(memory_space=pltpu.VMEM)
    local_copies = [
        (pltpu.SMEM if k < 2 else pltpu.VMEM)(a.shape, a.dtype) for k, a in enumerate(operands)
    ]
    limit = pltpu.CompilerParams(vmem_limit_bytes=20 * 1024 * 1024)
    partial = (
        jax.ShapeDtypeStruct((XN, ZN, NB, OR, LANES), F32),
        jax.ShapeDtypeStruct((XN, ZN, NB, OR, LANES), BF16),
    )
    across = pltpu.VMEM((2, NB, basis * RB, GW), BF16)
    keep, send = pl.pallas_call(
        compute_kernel,
        out_shape=partial,
        in_specs=[pl.BlockSpec(memory_space=pltpu.HBM)] * len(operands),
        out_specs=(vmem,) * 2,
        scratch_shapes=local_copies
        + [
            pltpu.VMEM((NB * RB, source.shape[3]), BF16),
            pltpu.VMEM((NB * RB, width + 2 * LANES), BF16),
            pltpu.VMEM((2 * LANES, basis * LANES), BF16),
            pltpu.VMEM((NB, 3 * OR, basis * RB), BF16),
            pltpu.VMEM((NB, coverage.shape[1], LANES), F32),
            across,
            pltpu.SemaphoreType.DMA((len(operands),)),
        ],
        compiler_params=limit,
    )(*(pltpu.with_memory_space_constraint(a, pltpu.HBM) for a in operands))

    both = keep + lax.ppermute(send, "visit", SIBLING).astype(F32)

    count = lax.axis_size("band")
    after = both[:, :, :, RB : RB + EDGE].astype(BF16)
    before = both[:, :, :, RB + EDGE :].astype(BF16)
    after = lax.ppermute(after, "band", [(i, (i + 1) % count) for i in range(count)])
    before = lax.ppermute(before, "band", [((i + 1) % count, i) for i in range(count)])
    own = both[:, :, :, :RB] + jnp.concatenate([after, before], axis=3).astype(F32)

    from_x = [
        lax.ppermute(own[d].astype(BF16), "visit", ACROSS_X[d - 1]) for d in range(1, XN)
    ]
    plane = own[0] + sum(part.astype(F32) for part in from_x)
    from_z = lax.all_to_all(
        plane.astype(BF16), "visit", 0, 0, axis_index_groups=ALONG_Z, tiled=True
    )
    return jnp.sum(from_z.astype(F32), axis=0)


def solution(mesh):
    in_specs = (
        P("visit", None, "band", None),
        P("visit", "band"),
        P("visit", None, "band"),
        P("visit", None),
        P("visit", None, None),
        P("visit", None),
        P(),
        P(),
        P(),
        P("visit", None),
        P(),
        P(),
    )
    out_specs = P(None, "band", "visit")
    return jax.shard_map(local, mesh=mesh, in_specs=in_specs, out_specs=out_specs, check_vma=False)
```

```python
import jax
import jax.numpy as jnp
from jax import lax
from jax.sharding import PartitionSpec as P
from jax.experimental import pallas as pl
from jax.experimental.pallas import tpu as pltpu

F32 = jnp.float32
I16 = jnp.int16
BF16 = jnp.bfloat16
HIGH = lax.Precision.HIGHEST

NB = 2
RB = 32
SR = 40
LANES = 128
ZN, XN, CN = 8, 4, 2
GROUP = XN * CN
GW = GROUP * LANES
EDGE = 16
OR = RB + 2 * EDGE
HALF = LANES // 2


def iota(shape, dim):
    return lax.broadcasted_iota(jnp.int32, shape, dim)


def mm(a, b):
    return jnp.dot(a, b, preferred_element_type=F32)


def compute_kernel(
    off_hbm,
    ids_hbm,
    source_hbm,
    row_start_hbm,
    row_weight_hbm,
    col_start_hbm,
    col_weight_hbm,
    g_hbm,
    h_hbm,
    coef_hbm,
    weight_hbm,
    cover_hbm,
    keep_ref,
    keep_edge_ref,
    send_ref,
    send_edge_ref,
    off_ref,
    ids_ref,
    source_ref,
    row_start_ref,
    row_weight_ref,
    col_start_ref,
    col_weight_ref,
    g_ref,
    h_ref,
    coef_ref,
    weight_ref,
    cover_ref,
    rowres_ref,
    shifted_ref,
    toep_ref,
    rows_ref,
    scale_ref,
    across_ref,
    sems,
):
    pairs = [
        (h_hbm, h_ref),
        (g_hbm, g_ref),
        (coef_hbm, coef_ref),
        (ids_hbm, ids_ref),
        (weight_hbm, weight_ref),
        (cover_hbm, cover_ref),
        (row_start_hbm, row_start_ref),
        (row_weight_hbm, row_weight_ref),
        (source_hbm, source_ref),
        (off_hbm, off_ref),
        (col_start_hbm, col_start_ref),
        (col_weight_hbm, col_weight_ref),
    ]
    copies = [pltpu.make_async_copy(a, b, sems.at[i]) for i, (a, b) in enumerate(pairs)]
    for copy in copies:
        copy.start()
    visit = lax.axis_index("visit")
    band = lax.axis_index("band")
    taps = g_ref.shape[1]
    margin = taps // 2
    basis = g_ref.shape[0]
    blocks = off_ref.shape[1]
    width = blocks * LANES
    visits = cover_ref.shape[0]

    for copy in copies[:6]:
        copy.wait()

    low_row, high_row = 48, 208
    tile = (high_row - low_row, LANES)
    tap = (iota(tile, 0) - iota(tile, 1) - (HALF - margin - low_row)).astype(I16)
    toep_ref[:low_row] = jnp.zeros((low_row, basis * LANES), BF16)
    toep_ref[high_row:] = jnp.zeros((2 * LANES - high_row, basis * LANES), BF16)
    h_all = h_ref[...].astype(F32)
    for b in range(basis):
        acc = jnp.zeros(tile, BF16)
        for t in range(taps):
            acc = jnp.where(
                tap == t, jnp.broadcast_to(h_all[b : b + 1, t : t + 1], tile).astype(BF16), acc
            )
        toep_ref[low_row:high_row, b * LANES : (b + 1) * LANES] = acc

    span = basis * RB
    repeat = (iota((basis, span), 1) // RB == iota((basis, span), 0)).astype(F32)
    g_wide = mm(g_ref[...].astype(F32).T.astype(BF16), repeat.astype(BF16))
    place = iota((OR, span), 0)
    out_row = jnp.where(place < RB + margin, place, place - OR)
    tap = iota((OR, span), 1) % RB - out_row + margin
    tract_row = band * RB + out_row
    valid = (place < RB + margin) | (place >= OR - margin)
    valid &= (tract_row >= 0) & (tract_row < RB * lax.axis_size("band"))
    g_taps = jnp.zeros((OR, span), F32)
    for t in range(taps):
        g_taps = jnp.where(tap == t, g_wide[t : t + 1, :], g_taps)
    g_taps = jnp.where(valid, g_taps, 0.0)
    y = (tract_row.astype(F32) + 0.5) * (2.0 / (RB * lax.axis_size("band"))) - 1.0
    for n in range(NB):
        table = coef_ref[:, pl.ds(ids_ref[0, n], 1), :].reshape(coef_ref.shape[0], basis)
        c = jnp.dot(table, repeat, precision=HIGH)
        in_x = [
            c[0:1] + c[2:3] * y + c[5:6] * (y * y),
            c[1:2] + c[4:5] * y,
            c[3:4] + jnp.zeros_like(y),
        ]
        for k in range(3):
            rows_ref[n, k * OR : (k + 1) * OR, :] = (g_taps * in_x[k]).astype(BF16)

    cover = cover_ref[...].astype(F32)
    mine = jnp.where(iota(cover.shape, 0) == visit, cover, 0.0)
    weight = weight_ref[...]
    dims = (((0,), (1,)), ((), ()))
    denom = lax.dot_general(cover, weight, dims, precision=HIGH)
    own = lax.dot_general(mine, weight, dims, precision=HIGH)
    factor = own / denom
    for n in range(NB):
        scale_ref[n] = jnp.broadcast_to(factor[:, n : n + 1], (visits, LANES))

    for copy in copies[6:]:
        copy.wait()

    start = row_start_ref[...]
    weights = row_weight_ref[0].astype(F32)
    rel = iota((SR, RB), 0) - start
    picked = jnp.zeros((SR, RB), F32)
    for q in range(4):
        picked = jnp.where(rel == q, weights[q : q + 1, :], picked)
    picker = picked.T.astype(BF16)
    chunk = 2 * LANES

    def row_step(j, _):
        cols = pl.ds(pl.multiple_of(j * chunk, chunk), chunk)
        for n in range(NB):
            rowres_ref[n * RB : (n + 1) * RB, cols] = mm(
                picker, source_ref[0, n, :, cols]
            ).astype(BF16)
        return 0

    lax.fori_loop(0, rowres_ref.shape[1] // chunk, row_step, 0, unroll=33)

    low = iota((NB * RB, 2 * LANES), 1) < HALF
    tall = 3 * LANES
    tall_iota = iota((tall, LANES), 0).astype(I16)

    def col_step(c, before):
        if c == blocks // 2:
            shifted_ref[:, c * 2 * LANES :] = jnp.where(low, before, 0.0).astype(BF16)
            return before
        spreads = []
        for k in range(2):
            cols = slice((2 * c + k) * LANES, (2 * c + k + 1) * LANES)
            at = col_start_ref[0:1, cols] + off_ref[0, 2 * c + k]
            wts = col_weight_ref[0, :, cols]
            rel = tall_iota - jnp.broadcast_to(at, (tall, LANES)).astype(I16)
            spread = jnp.zeros((tall, LANES), BF16)
            for q in range(4):
                spread = jnp.where(
                    rel == q, jnp.broadcast_to(wts[q : q + 1, :], (tall, LANES)), spread
                )
            spreads.append(spread)
        none = jnp.zeros((LANES, LANES), BF16)
        both = jnp.concatenate(
            [
                jnp.concatenate([spreads[0], none], axis=0),
                jnp.concatenate([none, spreads[1]], axis=0),
            ],
            axis=1,
        )
        first = c * 2 * LANES
        res = mm(rowres_ref[:, first : first + tall + LANES], both)
        rolled = pltpu.roll(res, HALF, 1)
        shifted_ref[:, first : first + 2 * LANES] = jnp.where(low, before, rolled).astype(BF16)
        return rolled

    core = visit % CN
    my_x = (visit // CN) % XN

    def window(z):
        return jnp.concatenate(
            [
                shifted_ref[:, (z * GROUP + k) * LANES : (z * GROUP + k + 2) * LANES]
                for k in range(GROUP)
            ],
            axis=0,
        )

    def filter_columns(z, lhs, pair):
        res = mm(lhs, toep_ref[:, pair * 2 * LANES : (pair + 1) * 2 * LANES]).astype(BF16)
        for k in range(GROUP):
            for n in range(NB):
                for b in range(2):
                    across_ref[
                        z % 2,
                        n,
                        (2 * pair + b) * RB : (2 * pair + b + 1) * RB,
                        k * LANES : (k + 1) * LANES,
                    ] = res[
                        (k * NB + n) * RB : (k * NB + n + 1) * RB,
                        b * LANES : (b + 1) * LANES,
                    ]

    def filter_rows(z, x, n):
        col = (z * GW + x * 2 * LANES + iota((1, 2 * LANES), 1)).astype(F32)
        xc = (col + 0.5) * (2.0 / width) - 1.0
        patch = z * GROUP + x * CN
        slot = my_x ^ x
        res = mm(rows_ref[n], across_ref[z % 2, n, :, x * 2 * LANES : (x + 1) * 2 * LANES])
        total = res[:OR] + xc * (res[OR : 2 * OR] + xc * res[2 * OR :])
        scale = jnp.concatenate(
            [scale_ref[n, patch + c : patch + c + 1, :] for c in range(CN)], axis=1
        )
        total = total * scale
        even, odd = total[:, :LANES], total[:, LANES:]
        keep = jnp.where(core == 0, even, odd)
        keep_ref[slot, z, n] = keep[:RB]
        keep_edge_ref[slot, z, n] = keep[RB:]
        send = jnp.where(core == 0, odd, even).astype(BF16)
        send_ref[slot, z, n] = send[:RB]
        send_edge_ref[slot, z, n] = send[RB:]

    before = jnp.zeros((NB * RB, 2 * LANES), F32)
    ready = GROUP // 2 + 1
    for c in range(ready):
        before = col_step(c, before)
    for z in range(ZN + 1):
        lhs = window(z) if z < ZN else None
        for step in range(GROUP):
            if z < ZN:
                filter_columns(z, lhs, step)
            if step % 2 == 0 and ready <= blocks // 2:
                before = col_step(ready, before)
                ready += 1
            if z > 0:
                filter_rows(z - 1, step // 2, step % 2)


def ring(step):
    return [(i, step(i // GROUP, (i // CN) % XN, i % CN)) for i in range(ZN * GROUP)]


def at(z, x, c):
    return (z % ZN) * GROUP + x * CN + c


SIBLING = ring(lambda z, x, c: at(z, x, c ^ 1))
ACROSS_X = [ring(lambda z, x, c, d=d: at(z, x ^ d, c)) for d in range(1, XN)]
ALONG_Z = [[at(z, x, c) for z in range(ZN)] for x in range(XN) for c in range(CN)]


def local(
    source,
    row_start,
    row_weight,
    col_start,
    col_weight,
    col_offset,
    g_taps,
    h_taps,
    coef_table,
    table_ids,
    vis_weight,
    coverage,
):
    basis = g_taps.shape[0]
    width = col_start.shape[1]
    operands = (
        col_offset,
        table_ids,
        source,
        row_start,
        row_weight,
        col_start,
        col_weight,
        g_taps,
        h_taps,
        coef_table.transpose(2, 0, 1),
        vis_weight.T,
        coverage,
    )
    vmem = pl.BlockSpec(memory_space=pltpu.VMEM)
    local_copies = [
        (pltpu.SMEM if k < 2 else pltpu.VMEM)(a.shape, a.dtype) for k, a in enumerate(operands)
    ]
    limit = pltpu.CompilerParams(vmem_limit_bytes=20 * 1024 * 1024)
    wide = jax.ShapeDtypeStruct((XN, ZN, NB, RB, LANES), F32)
    narrow = jax.ShapeDtypeStruct((XN, ZN, NB, RB, LANES), BF16)
    across = pltpu.VMEM((2, NB, basis * RB, GW), BF16)
    keep, keep_edge, send, send_edge = pl.pallas_call(
        compute_kernel,
        out_shape=(wide, wide, narrow, narrow),
        in_specs=[pl.BlockSpec(memory_space=pltpu.HBM)] * len(operands),
        out_specs=(vmem,) * 4,
        scratch_shapes=local_copies
        + [
            pltpu.VMEM((NB * RB, source.shape[3]), BF16),
            pltpu.VMEM((NB * RB, width + 2 * LANES), BF16),
            pltpu.VMEM((2 * LANES, basis * LANES), BF16),
            pltpu.VMEM((NB, 3 * OR, basis * RB), BF16),
            pltpu.VMEM((NB, coverage.shape[1], LANES), F32),
            across,
            pltpu.SemaphoreType.DMA((len(operands),)),
        ],
        compiler_params=limit,
    )(*(pltpu.with_memory_space_constraint(a, pltpu.HBM) for a in operands))

    edge = keep_edge + lax.ppermute(send_edge, "visit", SIBLING).astype(F32)
    count = lax.axis_size("band")
    after = edge[:, :, :, :EDGE].astype(BF16)
    before = edge[:, :, :, EDGE:].astype(BF16)
    after = lax.ppermute(after, "band", [(i, (i + 1) % count) for i in range(count)])
    before = lax.ppermute(before, "band", [((i + 1) % count, i) for i in range(count)])
    own = keep + lax.ppermute(send, "visit", SIBLING).astype(F32)
    own = own + jnp.concatenate([after, before], axis=3).astype(F32)

    from_x = [
        lax.ppermute(own[d].astype(BF16), "visit", ACROSS_X[d - 1]) for d in range(1, XN)
    ]
    plane = own[0] + sum(part.astype(F32) for part in from_x)
    from_z = lax.all_to_all(
        plane.astype(BF16), "visit", 0, 0, axis_index_groups=ALONG_Z, tiled=True
    )
    return jnp.sum(from_z.astype(F32), axis=0)


def solution(mesh):
    in_specs = (
        P("visit", None, "band", None),
        P("visit", "band"),
        P("visit", None, "band"),
        P("visit", None),
        P("visit", None, None),
        P("visit", None),
        P(),
        P(),
        P(),
        P("visit", None),
        P(),
        P(),
    )
    out_specs = P(None, "band", "visit")
    return jax.shard_map(local, mesh=mesh, in_specs=in_specs, out_specs=out_specs, check_vma=False)
```

```python
import jax
import jax.numpy as jnp
from jax import lax
from jax.sharding import PartitionSpec as P
from jax.experimental import pallas as pl
from jax.experimental.pallas import tpu as pltpu

F32 = jnp.float32
I16 = jnp.int16
BF16 = jnp.bfloat16
HIGH = lax.Precision.HIGHEST

NB = 2
RB = 32
SR = 40
LANES = 128
ZN, XN, CN = 8, 4, 2
GROUP = XN * CN
GW = GROUP * LANES
EDGE = 16
OR = RB + 2 * EDGE
HALF = LANES // 2


def iota(shape, dim):
    return lax.broadcasted_iota(jnp.int32, shape, dim)


def mm(a, b):
    return jnp.dot(a, b, preferred_element_type=F32)


def compute_kernel(
    off_hbm,
    ids_hbm,
    source_hbm,
    row_start_hbm,
    row_weight_hbm,
    col_start_hbm,
    col_weight_hbm,
    g_hbm,
    h_hbm,
    coef_hbm,
    weight_hbm,
    cover_hbm,
    keep_ref,
    keep_edge_ref,
    send_ref,
    send_edge_ref,
    off_ref,
    ids_ref,
    source_ref,
    row_start_ref,
    row_weight_ref,
    col_start_ref,
    col_weight_ref,
    g_ref,
    h_ref,
    coef_ref,
    weight_ref,
    cover_ref,
    rowres_ref,
    shifted_ref,
    toep_ref,
    rows_ref,
    scale_ref,
    across_ref,
    sems,
):
    pairs = [
        (h_hbm, h_ref),
        (g_hbm, g_ref),
        (coef_hbm, coef_ref),
        (ids_hbm, ids_ref),
        (weight_hbm, weight_ref),
        (cover_hbm, cover_ref),
        (row_start_hbm, row_start_ref),
        (row_weight_hbm, row_weight_ref),
        (source_hbm, source_ref),
        (off_hbm, off_ref),
        (col_start_hbm, col_start_ref),
        (col_weight_hbm, col_weight_ref),
    ]
    copies = [pltpu.make_async_copy(a, b, sems.at[i]) for i, (a, b) in enumerate(pairs)]
    for copy in copies:
        copy.start()
    visit = lax.axis_index("visit")
    band = lax.axis_index("band")
    taps = g_ref.shape[1]
    margin = taps // 2
    basis = g_ref.shape[0]
    blocks = off_ref.shape[1]
    width = blocks * LANES
    visits = cover_ref.shape[0]

    for copy in copies[:6]:
        copy.wait()

    low_row, high_row = 48, 208
    tile = (high_row - low_row, LANES)
    tap = (iota(tile, 0) - iota(tile, 1) - (HALF - margin - low_row)).astype(I16)
    toep_ref[:low_row] = jnp.zeros((low_row, basis * LANES), BF16)
    toep_ref[high_row:] = jnp.zeros((2 * LANES - high_row, basis * LANES), BF16)
    h_all = h_ref[...].astype(F32)
    for b in range(basis):
        acc = jnp.zeros(tile, BF16)
        for t in range(taps):
            acc = jnp.where(
                tap == t, jnp.broadcast_to(h_all[b : b + 1, t : t + 1], tile).astype(BF16), acc
            )
        toep_ref[low_row:high_row, b * LANES : (b + 1) * LANES] = acc

    span = basis * RB
    repeat = (iota((basis, span), 1) // RB == iota((basis, span), 0)).astype(F32)
    g_wide = mm(g_ref[...].astype(F32).T.astype(BF16), repeat.astype(BF16))
    place = iota((OR, span), 0)
    out_row = jnp.where(place < RB + margin, place, place - OR)
    tap = iota((OR, span), 1) % RB - out_row + margin
    tract_row = band * RB + out_row
    valid = (place < RB + margin) | (place >= OR - margin)
    valid &= (tract_row >= 0) & (tract_row < RB * lax.axis_size("band"))
    g_taps = jnp.zeros((OR, span), F32)
    for t in range(taps):
        g_taps = jnp.where(tap == t, g_wide[t : t + 1, :], g_taps)
    g_taps = jnp.where(valid, g_taps, 0.0)
    y = (tract_row.astype(F32) + 0.5) * (2.0 / (RB * lax.axis_size("band"))) - 1.0
    for n in range(NB):
        table = coef_ref[:, pl.ds(ids_ref[0, n], 1), :].reshape(coef_ref.shape[0], basis)
        c = jnp.dot(table, repeat, precision=HIGH)
        in_x = [
            c[0:1] + c[2:3] * y + c[5:6] * (y * y),
            c[1:2] + c[4:5] * y,
            c[3:4] + jnp.zeros_like(y),
        ]
        for k in range(3):
            rows_ref[n, k * OR : (k + 1) * OR, :] = (g_taps * in_x[k]).astype(BF16)

    cover = cover_ref[...].astype(F32)
    mine = jnp.where(iota(cover.shape, 0) == visit, cover, 0.0)
    weight = weight_ref[...]
    dims = (((0,), (1,)), ((), ()))
    denom = lax.dot_general(cover, weight, dims, precision=HIGH)
    own = lax.dot_general(mine, weight, dims, precision=HIGH)
    factor = own / denom
    for n in range(NB):
        scale_ref[n] = jnp.broadcast_to(factor[:, n : n + 1], (visits, LANES))

    for copy in copies[6:]:
        copy.wait()

    start = row_start_ref[...]
    weights = row_weight_ref[0].astype(F32)
    rel = iota((SR, RB), 0) - start
    picked = jnp.zeros((SR, RB), F32)
    for q in range(4):
        picked = jnp.where(rel == q, weights[q : q + 1, :], picked)
    picker = picked.T.astype(BF16)
    chunk = 2 * LANES

    def row_step(j, _):
        cols = pl.ds(pl.multiple_of(j * chunk, chunk), chunk)
        for n in range(NB):
            rowres_ref[n * RB : (n + 1) * RB, cols] = mm(
                picker, source_ref[0, n, :, cols]
            ).astype(BF16)
        return 0

    lax.fori_loop(0, rowres_ref.shape[1] // chunk, row_step, 0, unroll=33)

    low = iota((NB * RB, 2 * LANES), 1) < HALF
    tall = 3 * LANES
    tall_iota = iota((tall, LANES), 0).astype(I16)

    def col_step(c, before):
        if c == blocks // 2:
            shifted_ref[:, c * 2 * LANES :] = jnp.where(low, before, 0.0).astype(BF16)
            return before
        spreads = []
        for k in range(2):
            cols = slice((2 * c + k) * LANES, (2 * c + k + 1) * LANES)
            at = col_start_ref[0:1, cols] + off_ref[0, 2 * c + k]
            wts = col_weight_ref[0, :, cols]
            rel = tall_iota - jnp.broadcast_to(at, (tall, LANES)).astype(I16)
            spread = jnp.zeros((tall, LANES), BF16)
            for q in range(4):
                spread = jnp.where(
                    rel == q, jnp.broadcast_to(wts[q : q + 1, :], (tall, LANES)), spread
                )
            spreads.append(spread)
        none = jnp.zeros((LANES, LANES), BF16)
        both = jnp.concatenate(
            [
                jnp.concatenate([spreads[0], none], axis=0),
                jnp.concatenate([none, spreads[1]], axis=0),
            ],
            axis=1,
        )
        first = c * 2 * LANES
        res = mm(rowres_ref[:, first : first + tall + LANES], both)
        rolled = pltpu.roll(res, HALF, 1)
        shifted_ref[:, first : first + 2 * LANES] = jnp.where(low, before, rolled).astype(BF16)
        return rolled

    core = visit % CN
    my_x = (visit // CN) % XN

    def window(z):
        return jnp.concatenate(
            [
                shifted_ref[:, (z * GROUP + k) * LANES : (z * GROUP + k + 2) * LANES]
                for k in range(GROUP)
            ],
            axis=0,
        )

    def filter_columns(z, lhs, pair):
        res = mm(lhs, toep_ref[:, pair * 2 * LANES : (pair + 1) * 2 * LANES]).astype(BF16)
        for k in range(GROUP):
            for n in range(NB):
                for b in range(2):
                    across_ref[
                        z % 2,
                        n,
                        (2 * pair + b) * RB : (2 * pair + b + 1) * RB,
                        k * LANES : (k + 1) * LANES,
                    ] = res[
                        (k * NB + n) * RB : (k * NB + n + 1) * RB,
                        b * LANES : (b + 1) * LANES,
                    ]

    def filter_rows(z, x, n):
        col = (z * GW + x * 2 * LANES + iota((1, 2 * LANES), 1)).astype(F32)
        xc = (col + 0.5) * (2.0 / width) - 1.0
        patch = z * GROUP + x * CN
        slot = my_x ^ x
        res = mm(rows_ref[n], across_ref[z % 2, n, :, x * 2 * LANES : (x + 1) * 2 * LANES])
        total = res[:OR] + xc * (res[OR : 2 * OR] + xc * res[2 * OR :])
        scale = jnp.concatenate(
            [scale_ref[n, patch + c : patch + c + 1, :] for c in range(CN)], axis=1
        )
        total = total * scale
        even, odd = total[:, :LANES], total[:, LANES:]
        keep = jnp.where(core == 0, even, odd)
        keep_ref[slot, z, n] = keep[:RB]
        keep_edge_ref[slot, z, n] = keep[RB:]
        send = jnp.where(core == 0, odd, even).astype(BF16)
        send_ref[slot, z, n] = send[:RB]
        send_edge_ref[slot, z, n] = send[RB:]

    before = jnp.zeros((NB * RB, 2 * LANES), F32)
    ready = GROUP // 2 + 1
    for c in range(ready):
        before = col_step(c, before)
    for z in range(ZN + 1):
        lhs = window(z) if z < ZN else None
        for step in range(GROUP):
            if z < ZN:
                filter_columns(z, lhs, step)
            if step % 2 == 0 and ready <= blocks // 2:
                before = col_step(ready, before)
                ready += 1
            if z > 0:
                filter_rows(z - 1, step // 2, step % 2)


def ring(step):
    return [(i, step(i // GROUP, (i // CN) % XN, i % CN)) for i in range(ZN * GROUP)]


def at(z, x, c):
    return (z % ZN) * GROUP + x * CN + c


SIBLING = ring(lambda z, x, c: at(z, x, c ^ 1))
ACROSS_X = [ring(lambda z, x, c, d=d: at(z, x ^ d, c)) for d in range(1, XN)]
ALONG_Z = [[at(z, x, c) for z in range(ZN)] for x in range(XN) for c in range(CN)]


def local(
    source,
    row_start,
    row_weight,
    col_start,
    col_weight,
    col_offset,
    g_taps,
    h_taps,
    coef_table,
    table_ids,
    vis_weight,
    coverage,
):
    basis = g_taps.shape[0]
    width = col_start.shape[1]
    operands = (
        col_offset,
        table_ids,
        source,
        row_start,
        row_weight,
        col_start,
        col_weight,
        g_taps,
        h_taps,
        coef_table.transpose(2, 0, 1),
        vis_weight.T,
        coverage,
    )
    vmem = pl.BlockSpec(memory_space=pltpu.VMEM)
    local_copies = [
        (pltpu.SMEM if k < 2 else pltpu.VMEM)(a.shape, a.dtype) for k, a in enumerate(operands)
    ]
    limit = pltpu.CompilerParams(vmem_limit_bytes=20 * 1024 * 1024)
    wide = jax.ShapeDtypeStruct((XN, ZN, NB, RB, LANES), F32)
    narrow = jax.ShapeDtypeStruct((XN, ZN, NB, RB, LANES), BF16)
    across = pltpu.VMEM((2, NB, basis * RB, GW), BF16)
    keep, keep_edge, send, send_edge = pl.pallas_call(
        compute_kernel,
        out_shape=(wide, wide, narrow, narrow),
        in_specs=[pl.BlockSpec(memory_space=pltpu.HBM)] * len(operands),
        out_specs=(vmem,) * 4,
        scratch_shapes=local_copies
        + [
            pltpu.VMEM((NB * RB, source.shape[3]), BF16),
            pltpu.VMEM((NB * RB, width + 2 * LANES), BF16),
            pltpu.VMEM((2 * LANES, basis * LANES), BF16),
            pltpu.VMEM((NB, 3 * OR, basis * RB), BF16),
            pltpu.VMEM((NB, coverage.shape[1], LANES), F32),
            across,
            pltpu.SemaphoreType.DMA((len(operands),)),
        ],
        compiler_params=limit,
    )(*(pltpu.with_memory_space_constraint(a, pltpu.HBM) for a in operands))

    edge = keep_edge + lax.ppermute(send_edge, "visit", SIBLING).astype(F32)
    count = lax.axis_size("band")

    def along_y(rows):
        after = rows[:, :, :, :EDGE].astype(BF16)
        before = rows[:, :, :, EDGE:].astype(BF16)
        after = lax.ppermute(after, "band", [(i, (i + 1) % count) for i in range(count)])
        before = lax.ppermute(before, "band", [((i + 1) % count, i) for i in range(count)])
        return jnp.concatenate([after, before], axis=3).astype(F32)

    moving = along_y(edge[1:])
    staying = along_y(edge[:1])
    own = keep + lax.ppermute(send, "visit", SIBLING).astype(F32)
    moving = (own[1:] + moving).astype(BF16)

    from_x = [lax.ppermute(moving[d - 1], "visit", ACROSS_X[d - 1]) for d in range(1, XN)]
    plane = own[0] + staying[0] + sum(part.astype(F32) for part in from_x)
    from_z = lax.all_to_all(
        plane.astype(BF16), "visit", 0, 0, axis_index_groups=ALONG_Z, tiled=True
    )
    return jnp.sum(from_z.astype(F32), axis=0)


def solution(mesh):
    in_specs = (
        P("visit", None, "band", None),
        P("visit", "band"),
        P("visit", None, "band"),
        P("visit", None),
        P("visit", None, None),
        P("visit", None),
        P(),
        P(),
        P(),
        P("visit", None),
        P(),
        P(),
    )
    out_specs = P(None, "band", "visit")
    return jax.shard_map(local, mesh=mesh, in_specs=in_specs, out_specs=out_specs, check_vma=False)
```

```python
import jax
import jax.numpy as jnp
from jax import lax
from jax.sharding import PartitionSpec as P
from jax.experimental import pallas as pl
from jax.experimental.pallas import tpu as pltpu

F32 = jnp.float32
I16 = jnp.int16
BF16 = jnp.bfloat16
HIGH = lax.Precision.HIGHEST

NB = 2
RB = 32
SR = 40
LANES = 128
ZN, XN, CN = 8, 4, 2
GROUP = XN * CN
GW = GROUP * LANES
EDGE = 16
OR = RB + 2 * EDGE
HALF = LANES // 2


def iota(shape, dim):
    return lax.broadcasted_iota(jnp.int32, shape, dim)


def mm(a, b):
    return jnp.dot(a, b, preferred_element_type=F32)


def compute_kernel(
    off_hbm,
    ids_hbm,
    source_hbm,
    row_start_hbm,
    row_weight_hbm,
    col_start_hbm,
    col_weight_hbm,
    g_hbm,
    h_hbm,
    coef_hbm,
    weight_hbm,
    cover_hbm,
    keep_ref,
    keep_edge_ref,
    send_ref,
    send_edge_ref,
    off_ref,
    ids_ref,
    source_ref,
    row_start_ref,
    row_weight_ref,
    col_start_ref,
    col_weight_ref,
    g_ref,
    h_ref,
    coef_ref,
    weight_ref,
    cover_ref,
    rowres_ref,
    shifted_ref,
    toep_ref,
    rows_ref,
    scale_ref,
    across_ref,
    sems,
):
    pairs = [
        (h_hbm, h_ref),
        (g_hbm, g_ref),
        (coef_hbm, coef_ref),
        (ids_hbm, ids_ref),
        (weight_hbm, weight_ref),
        (cover_hbm, cover_ref),
        (row_start_hbm, row_start_ref),
        (row_weight_hbm, row_weight_ref),
        (source_hbm, source_ref),
        (off_hbm, off_ref),
        (col_start_hbm, col_start_ref),
        (col_weight_hbm, col_weight_ref),
    ]
    copies = [pltpu.make_async_copy(a, b, sems.at[i]) for i, (a, b) in enumerate(pairs)]
    for copy in copies:
        copy.start()
    visit = lax.axis_index("visit")
    band = lax.axis_index("band")
    taps = g_ref.shape[1]
    margin = taps // 2
    basis = g_ref.shape[0]
    blocks = off_ref.shape[1]
    width = blocks * LANES
    visits = cover_ref.shape[0]

    for copy in copies[:6]:
        copy.wait()

    low_row, high_row = 48, 208
    tile = (high_row - low_row, LANES)
    tap = (iota(tile, 0) - iota(tile, 1) - (HALF - margin - low_row)).astype(I16)
    toep_ref[:low_row] = jnp.zeros((low_row, basis * LANES), BF16)
    toep_ref[high_row:] = jnp.zeros((2 * LANES - high_row, basis * LANES), BF16)
    h_all = h_ref[...].astype(F32)
    for b in range(basis):
        acc = jnp.zeros(tile, BF16)
        for t in range(taps):
            acc = jnp.where(
                tap == t, jnp.broadcast_to(h_all[b : b + 1, t : t + 1], tile).astype(BF16), acc
            )
        toep_ref[low_row:high_row, b * LANES : (b + 1) * LANES] = acc

    span = basis * RB
    repeat = (iota((basis, span), 1) // RB == iota((basis, span), 0)).astype(F32)
    g_wide = mm(g_ref[...].astype(F32).T.astype(BF16), repeat.astype(BF16))
    place = iota((OR, span), 0)
    out_row = jnp.where(place < RB + margin, place, place - OR)
    tap = iota((OR, span), 1) % RB - out_row + margin
    tract_row = band * RB + out_row
    valid = (place < RB + margin) | (place >= OR - margin)
    valid &= (tract_row >= 0) & (tract_row < RB * lax.axis_size("band"))
    g_taps = jnp.zeros((OR, span), F32)
    for t in range(taps):
        g_taps = jnp.where(tap == t, g_wide[t : t + 1, :], g_taps)
    g_taps = jnp.where(valid, g_taps, 0.0)
    y = (tract_row.astype(F32) + 0.5) * (2.0 / (RB * lax.axis_size("band"))) - 1.0
    for n in range(NB):
        table = coef_ref[:, pl.ds(ids_ref[0, n], 1), :].reshape(coef_ref.shape[0], basis)
        c = jnp.dot(table, repeat, precision=HIGH)
        in_x = [
            c[0:1] + c[2:3] * y + c[5:6] * (y * y),
            c[1:2] + c[4:5] * y,
            c[3:4] + jnp.zeros_like(y),
        ]
        for k in range(3):
            rows_ref[n, k * OR : (k + 1) * OR, :] = (g_taps * in_x[k]).astype(BF16)

    cover = cover_ref[...].astype(F32)
    mine = jnp.where(iota(cover.shape, 0) == visit, cover, 0.0)
    weight = weight_ref[...]
    dims = (((0,), (1,)), ((), ()))
    denom = lax.dot_general(cover, weight, dims, precision=HIGH)
    own = lax.dot_general(mine, weight, dims, precision=HIGH)
    factor = own / denom
    for n in range(NB):
        scale_ref[n] = jnp.broadcast_to(factor[:, n : n + 1], (visits, LANES))

    for copy in copies[6:]:
        copy.wait()

    start = row_start_ref[...]
    weights = row_weight_ref[0].astype(F32)
    rel = iota((SR, RB), 0) - start
    picked = jnp.zeros((SR, RB), F32)
    for q in range(4):
        picked = jnp.where(rel == q, weights[q : q + 1, :], picked)
    picker = picked.T.astype(BF16)
    chunk = 2 * LANES

    def row_step(j, _):
        cols = pl.ds(pl.multiple_of(j * chunk, chunk), chunk)
        for n in range(NB):
            rowres_ref[n * RB : (n + 1) * RB, cols] = mm(
                picker, source_ref[0, n, :, cols]
            ).astype(BF16)
        return 0

    lax.fori_loop(0, rowres_ref.shape[1] // chunk, row_step, 0, unroll=33)

    low = iota((NB * RB, 2 * LANES), 1) < HALF
    tall = 3 * LANES
    tall_iota = iota((tall, LANES), 0).astype(I16)

    def col_step(c, before):
        if c == blocks // 2:
            shifted_ref[:, c * 2 * LANES :] = jnp.where(low, before, 0.0).astype(BF16)
            return before
        spreads = []
        for k in range(2):
            cols = slice((2 * c + k) * LANES, (2 * c + k + 1) * LANES)
            at = col_start_ref[0:1, cols] + off_ref[0, 2 * c + k]
            wts = col_weight_ref[0, :, cols]
            rel = tall_iota - jnp.broadcast_to(at, (tall, LANES)).astype(I16)
            spread = jnp.zeros((tall, LANES), BF16)
            for q in range(4):
                spread = jnp.where(
                    rel == q, jnp.broadcast_to(wts[q : q + 1, :], (tall, LANES)), spread
                )
            spreads.append(spread)
        none = jnp.zeros((LANES, LANES), BF16)
        both = jnp.concatenate(
            [
                jnp.concatenate([spreads[0], none], axis=0),
                jnp.concatenate([none, spreads[1]], axis=0),
            ],
            axis=1,
        )
        first = c * 2 * LANES
        res = mm(rowres_ref[:, first : first + tall + LANES], both)
        rolled = pltpu.roll(res, HALF, 1)
        shifted_ref[:, first : first + 2 * LANES] = jnp.where(low, before, rolled).astype(BF16)
        return rolled

    core = visit % CN
    my_x = (visit // CN) % XN

    def window(z):
        return jnp.concatenate(
            [
                shifted_ref[:, (z * GROUP + k) * LANES : (z * GROUP + k + 2) * LANES]
                for k in range(GROUP)
            ],
            axis=0,
        )

    def filter_columns(z, lhs, pair):
        res = mm(lhs, toep_ref[:, pair * 2 * LANES : (pair + 1) * 2 * LANES]).astype(BF16)
        for k in range(GROUP):
            for n in range(NB):
                for b in range(2):
                    across_ref[
                        z % 2,
                        n,
                        (2 * pair + b) * RB : (2 * pair + b + 1) * RB,
                        k * LANES : (k + 1) * LANES,
                    ] = res[
                        (k * NB + n) * RB : (k * NB + n + 1) * RB,
                        b * LANES : (b + 1) * LANES,
                    ]

    def filter_rows(z, x, n):
        col = (z * GW + x * 2 * LANES + iota((1, 2 * LANES), 1)).astype(F32)
        xc = (col + 0.5) * (2.0 / width) - 1.0
        patch = z * GROUP + x * CN
        slot = my_x ^ x
        res = mm(rows_ref[n], across_ref[z % 2, n, :, x * 2 * LANES : (x + 1) * 2 * LANES])
        total = res[:OR] + xc * (res[OR : 2 * OR] + xc * res[2 * OR :])
        scale = jnp.concatenate(
            [scale_ref[n, patch + c : patch + c + 1, :] for c in range(CN)], axis=1
        )
        total = total * scale
        even, odd = total[:, :LANES], total[:, LANES:]
        keep = jnp.where(core == 0, even, odd)
        keep_ref[slot, z, n] = keep[:RB]
        keep_edge_ref[slot, z, n] = keep[RB:]
        send = jnp.where(core == 0, odd, even).astype(BF16)
        send_ref[slot, z, n] = send[:RB]
        send_edge_ref[slot, z, n] = send[RB:]

    before = jnp.zeros((NB * RB, 2 * LANES), F32)
    ready = GROUP // 2 + 1
    for c in range(ready):
        before = col_step(c, before)
    for z in range(ZN + 1):
        lhs = window(z) if z < ZN else None
        for step in range(GROUP):
            if z < ZN:
                filter_columns(z, lhs, step)
            if step < GROUP // 2 and ready <= blocks // 2:
                before = col_step(ready, before)
                ready += 1
            if z > 0:
                filter_rows(z - 1, step // 2, step % 2)


def ring(step):
    return [(i, step(i // GROUP, (i // CN) % XN, i % CN)) for i in range(ZN * GROUP)]


def at(z, x, c):
    return (z % ZN) * GROUP + x * CN + c


SIBLING = ring(lambda z, x, c: at(z, x, c ^ 1))
ACROSS_X = [ring(lambda z, x, c, d=d: at(z, x ^ d, c)) for d in range(1, XN)]
ALONG_Z = [[at(z, x, c) for z in range(ZN)] for x in range(XN) for c in range(CN)]


def local(
    source,
    row_start,
    row_weight,
    col_start,
    col_weight,
    col_offset,
    g_taps,
    h_taps,
    coef_table,
    table_ids,
    vis_weight,
    coverage,
):
    basis = g_taps.shape[0]
    width = col_start.shape[1]
    operands = (
        col_offset,
        table_ids,
        source,
        row_start,
        row_weight,
        col_start,
        col_weight,
        g_taps,
        h_taps,
        coef_table.transpose(2, 0, 1),
        vis_weight.T,
        coverage,
    )
    vmem = pl.BlockSpec(memory_space=pltpu.VMEM)
    local_copies = [
        (pltpu.SMEM if k < 2 else pltpu.VMEM)(a.shape, a.dtype) for k, a in enumerate(operands)
    ]
    limit = pltpu.CompilerParams(vmem_limit_bytes=20 * 1024 * 1024)
    wide = jax.ShapeDtypeStruct((XN, ZN, NB, RB, LANES), F32)
    narrow = jax.ShapeDtypeStruct((XN, ZN, NB, RB, LANES), BF16)
    across = pltpu.VMEM((2, NB, basis * RB, GW), BF16)
    keep, keep_edge, send, send_edge = pl.pallas_call(
        compute_kernel,
        out_shape=(wide, wide, narrow, narrow),
        in_specs=[pl.BlockSpec(memory_space=pltpu.HBM)] * len(operands),
        out_specs=(vmem,) * 4,
        scratch_shapes=local_copies
        + [
            pltpu.VMEM((NB * RB, source.shape[3]), BF16),
            pltpu.VMEM((NB * RB, width + 2 * LANES), BF16),
            pltpu.VMEM((2 * LANES, basis * LANES), BF16),
            pltpu.VMEM((NB, 3 * OR, basis * RB), BF16),
            pltpu.VMEM((NB, coverage.shape[1], LANES), F32),
            across,
            pltpu.SemaphoreType.DMA((len(operands),)),
        ],
        compiler_params=limit,
    )(*(pltpu.with_memory_space_constraint(a, pltpu.HBM) for a in operands))

    edge = keep_edge + lax.ppermute(send_edge, "visit", SIBLING).astype(F32)
    count = lax.axis_size("band")

    def along_y(rows):
        after = rows[:, :, :, :EDGE].astype(BF16)
        before = rows[:, :, :, EDGE:].astype(BF16)
        after = lax.ppermute(after, "band", [(i, (i + 1) % count) for i in range(count)])
        before = lax.ppermute(before, "band", [((i + 1) % count, i) for i in range(count)])
        return jnp.concatenate([after, before], axis=3).astype(F32)

    moving = along_y(edge[1:])
    staying = along_y(edge[:1])
    own = keep + lax.ppermute(send, "visit", SIBLING).astype(F32)
    moving = (own[1:] + moving).astype(BF16)

    from_x = [lax.ppermute(moving[d - 1], "visit", ACROSS_X[d - 1]) for d in range(1, XN)]
    plane = own[0] + staying[0] + sum(part.astype(F32) for part in from_x)
    from_z = lax.all_to_all(
        plane.astype(BF16), "visit", 0, 0, axis_index_groups=ALONG_Z, tiled=True
    )
    return jnp.sum(from_z.astype(F32), axis=0)


def solution(mesh):
    in_specs = (
        P("visit", None, "band", None),
        P("visit", "band"),
        P("visit", None, "band"),
        P("visit", None),
        P("visit", None, None),
        P("visit", None),
        P(),
        P(),
        P(),
        P("visit", None),
        P(),
        P(),
    )
    out_specs = P(None, "band", "visit")
    return jax.shard_map(local, mesh=mesh, in_specs=in_specs, out_specs=out_specs, check_vma=False)
```
